32 devices in a mesh: pair: 2 (over y), tm: 16 (over z, x, core).
Axes of the slice: x: 2, y: 2, z: 4, core: 2. Of those that a mesh axis runs over, the one named last changes fastest.
Arguments:
- fields: float32 [2, 16, 256, 256], P('pair', 'tm'), may hold values from -4 to 4
- forcing: float32 [2, 16, 256, 256], P('pair', 'tm'), may hold values from -4 to 4.3
- diffusion: float32 [256, 256], replicated, may hold values from 0.5 to 2
- reaction: float32 [256, 256], replicated, may hold values from 0.02 to 0.2
- wrap_factor: float32 [1], replicated, may hold values from 0.05 to 0.4
- mean_diffusion: float32 [1], replicated, may hold values from 0.8 to 1.25
- spectral_shift: float32 [1], replicated, may hold values from 0.05 to 1
Outputs:
- updated: float32 [2, 16, 256, 256], P('pair', 'tm')
The draws below stay inside these ranges and needn't reach their ends.
All inputs are finite; a program needn't handle non-finite values.
Results may differ from the reference program's by a relative error of at most 0.0003.
Values sent between devices are 32-bit elements; how exact they have to be, the bound alone decides.
No kernel may reach another device: no remote copies, remote signals or barrier semaphores. Data moves between devices by JAX's collectives and lax.ppermute only.
A program may use at most 64 MiB of HBM per device.

```python
import math
import jax
import jax.numpy as jnp
from jax import lax

NX = 256
NY = 256
ITERS = 2
NT = 16


def draw_forcing(key, part):
    base = jnp.clip(jax.random.normal(key, (2, NT, NX, NY), jnp.float32), -4.0, 4.0)
    return base


def steps_of(rng, shape, pieces, least, high):
    def one(dim, blocks):
        heights = jax.random.uniform(jax.random.fold_in(jax.random.fold_in(rng, 6), dim), (blocks,), jnp.float32, least / len(pieces), high / len(pieces))
        return jnp.repeat(jnp.exp(heights), shape[dim] // blocks).reshape((-1,) + (1,) * (len(shape) - dim - 1))

    loudness = one(*pieces[0])
    for cut in pieces[1:]:
        loudness = loudness * one(*cut)
    return loudness


def bell_draw(own_key, extent, deviation, reach, split=(), kind=jnp.bfloat16):
    entries = jax.random.normal(own_key, extent, jnp.float32) * deviation
    if len(split) > 0:
        entries = steps_of(own_key, extent, split, -0.22, 0.18) * entries
    return jnp.clip(entries, min=-reach, max=reach).astype(kind)


def setup_inputs(seed: int = 0) -> dict:
    seeds = jax.random.split(jax.random.key(seed), 8)
    fields = bell_draw(seeds[0], (2, NT, NX, NY), 1.0, 4.0, ((0, 2), (1, 16)), jnp.float32)
    forcing = draw_forcing(jax.random.fold_in(seeds[7], 71), 0)
    diffusion = jnp.clip(jnp.exp(jax.random.uniform(seeds[2], (NX, NY), jnp.float32, math.log(0.5), math.log(2.0))), 0.5, 2.0)
    reaction = jnp.clip(jnp.exp(jax.random.uniform(seeds[3], (NX, NY), jnp.float32, math.log(0.02), math.log(0.2))), 0.02, 0.2)
    wrap_factor = jnp.clip(jax.random.uniform(seeds[4], (1,), jnp.float32, 0.05, 0.4), 0.05, 0.4)
    mean_diffusion = jnp.clip(jax.random.uniform(seeds[5], (1,), jnp.float32, 0.8, 1.25), 0.8, 1.25)
    spectral_shift = jnp.clip(jnp.exp(jax.random.uniform(seeds[6], (1,), jnp.float32, math.log(0.05), math.log(1.0))), 0.05, 1.0)
    return {"fields": fields, "forcing": forcing, "diffusion": diffusion, "reaction": reaction, "wrap_factor": wrap_factor, "mean_diffusion": mean_diffusion, "spectral_shift": spectral_shift}


gamma_inv = 0.5
step_rate = 1.0


def face_weights(diffusion):
    east_face = 0.5 * (diffusion + jnp.roll(diffusion, -1, 0))
    north_face = 0.5 * (diffusion + jnp.roll(diffusion, -1, 1))
    return east_face, north_face


def transport(values, east_face, north_face):
    flux_x = east_face * (jnp.roll(values, -1, -2) - values)
    flux_y = north_face * (jnp.roll(values, -1, -1) - values)
    return flux_x - jnp.roll(flux_x, 1, -2) + flux_y - jnp.roll(flux_y, 1, -1)


def residual_terms(own_field, earlier, partner, source, spread, reaction, adjoint_flag):
    state_coupling = reaction * own_field * own_field * own_field + gamma_inv * partner
    adjoint_coupling = 3.0 * reaction * partner * partner * own_field - partner
    coupling = jnp.where(adjoint_flag, adjoint_coupling, state_coupling)
    return source - ((own_field - earlier) * step_rate - spread + coupling)


def time_parts(mode_ids, total, log_alpha):
    ratio = jnp.exp(log_alpha / total)
    angles = (mode_ids % total).astype(jnp.float32) * (2.0 * math.pi / total)
    return step_rate * (1.0 - ratio * jnp.cos(angles)), step_rate * ratio * jnp.sin(angles)


def space_eigen(row_ids, col_ids, width_x, width_y):
    sine_rows = jnp.sin(row_ids.astype(jnp.float32) * (math.pi / width_x))
    sine_cols = jnp.sin(col_ids.astype(jnp.float32) * (math.pi / width_y))
    return 4.0 * sine_rows[:, None] ** 2 + 4.0 * sine_cols[None, :] ** 2


def reference(fields, forcing, diffusion, reaction, wrap_factor, mean_diffusion, spectral_shift):
    east_face, north_face = face_weights(diffusion)
    log_alpha = jnp.log(wrap_factor[0])
    time_ids = jnp.arange(NT, dtype=jnp.int32)
    time_scale = jnp.exp(time_ids.astype(jnp.float32) * (log_alpha / NT))
    time_re, time_im = time_parts(time_ids, NT, log_alpha)
    eigenvalue = space_eigen(jnp.arange(NX, dtype=jnp.int32), jnp.arange(NY, dtype=jnp.int32), NX, NY)
    den_re = time_re[:, None, None] + (mean_diffusion[0] * eigenvalue + spectral_shift[0])
    den_im = jnp.broadcast_to(time_im[:, None, None], den_re.shape)
    divisor = lax.complex(den_re, den_im)
    state_field = fields[0]
    adjoint = fields[1]
    zero_step = jnp.zeros((1, NX, NY), jnp.float32)
    for iteration in range(ITERS):
        new_pair = []
        for group_id, members in enumerate(((state_field, adjoint), (adjoint, state_field))):
            own_field, other_field = members
            if group_id == 0:
                earlier = jnp.concatenate([zero_step, own_field[:-1]], 0)
            else:
                earlier = jnp.concatenate([own_field[1:], zero_step], 0)
            spread = transport(own_field, east_face, north_face)
            residual = residual_terms(own_field, earlier, other_field, forcing[group_id], spread, reaction, group_id == 1)
            if group_id == 1:
                residual = jnp.flip(residual, 0)
            spectrum = jnp.fft.fftn(residual * time_scale[:, None, None])
            correction = jnp.fft.ifftn(spectrum / divisor).real / time_scale[:, None, None]
            if group_id == 1:
                correction = jnp.flip(correction, 0)
            new_pair.append(own_field + correction)
        state_field, adjoint = new_pair
    return jnp.stack([state_field, adjoint])
```

```python
import functools

import jax
import jax.numpy as jnp
import ml_dtypes
import numpy as np
from jax import lax
from jax.experimental import pallas as pl
from jax.experimental.pallas import tpu as pltpu
from jax.sharding import PartitionSpec as P

gamma_inv = 0.5
AXES = ("pair", "tm")


def cas_table(length):
    places = np.arange(length)
    angles = (places[:, None] * places[None, :] % length) * (2.0 * np.pi / length)
    table = np.cos(angles) + np.sin(angles)
    high = table.astype(ml_dtypes.bfloat16)
    low = (table - high.astype(np.float64)).astype(ml_dtypes.bfloat16)
    return jnp.asarray(high), jnp.asarray(low)


def split(values):
    high = values.astype(jnp.bfloat16)
    return high, (values - high.astype(jnp.float32)).astype(jnp.bfloat16)


def product(left, right, left_dim, right_dim):
    dims = (((left_dim,), (right_dim,)), ((), ()))

    def one(a, b):
        return lax.dot_general(a, b, dims, preferred_element_type=jnp.float32)

    return one(left[0], right[0]) + (one(left[0], right[1]) + one(left[1], right[0]))


def roll(values, shift, axis):
    return pltpu.roll(values, shift % values.shape[axis], axis)


def first_kernel(
    mean_ref, shift_ref, alpha_ref, pair_ref,
    own_ref, partner_ref, wrap_ref, source_ref, diffusion_ref, reaction_ref, high_ref, low_ref,
    out_ref,
):
    mean, shift, alpha = mean_ref[0], shift_ref[0], alpha_ref[0]
    cells = diffusion_ref[...]
    own, partner, reaction = own_ref[...], partner_ref[...], reaction_ref[...]
    east = 0.5 * (cells + roll(cells, -1, 0)) - mean
    north = 0.5 * (cells + roll(cells, -1, 1)) - mean
    flux_x = east * (roll(own, -1, 0) - own)
    flux_y = north * (roll(own, -1, 1) - own)
    spread = flux_x - roll(flux_x, 1, 0) + flux_y - roll(flux_y, 1, 1)
    adjoint = pair_ref[0] == 1
    state_coupling = reaction * own * own * own + gamma_inv * partner
    adjoint_coupling = 3.0 * reaction * partner * partner * own - partner
    coupling = jnp.where(adjoint, adjoint_coupling, state_coupling)
    side = source_ref[...] + (spread + shift * own - coupling) - alpha * wrap_ref[...]
    out_ref[...] = product((high_ref[...], low_ref[...]), split(side), 1, 1)


def solve_steps(rows, total, scale, rate, alpha, last_ref, work_ref, keep_ref):
    power = rate
    for _ in range(total - 1):
        power = power * rate
    gain = alpha / (1.0 - alpha * power)
    for group in range(2):
        order = range(total) if group == 0 else range(total - 1, -1, -1)
        places = [slice((group * total + step) * rows, (group * total + step + 1) * rows) for step in order]
        value = jnp.zeros_like(rate)
        for place in places:
            scaled = work_ref[place, :] * scale
            work_ref[place, :] = scaled
            value = rate * (value + scaled)
        if last_ref is not None:
            value = value - last_ref[group * rows : (group + 1) * rows, :]
        value = gain * value
        for place in places:
            value = rate * (value + work_ref[place, :])
            work_ref[place, :] = value
        if keep_ref is not None:
            keep_ref[group * rows : (group + 1) * rows, :] = value


def middle_kernel(rows, total, scale, alpha_ref, in_ref, rate_ref, high_ref, low_ref, out_ref, keep_ref, work_ref):
    table = (high_ref[...], low_ref[...])
    work_ref[...] = product(split(in_ref[...]), table, 1, 0)
    solve_steps(rows, total, scale, rate_ref[...], alpha_ref[0], None, work_ref, keep_ref)
    fields = product(split(work_ref[...]), table, 1, 0)
    band = rows * total
    half = fields.shape[1] // 2
    lane = lax.broadcasted_iota(jnp.int32, (band, half), 1)
    ends = (lane == 0) | (lane == half - 1)
    for side in range(2):
        inner = slice(side * half, (side + 1) * half)
        other = slice((1 - side) * half, (2 - side) * half)
        place = slice(side * band, (side + 1) * band)
        out_ref[place, :half] = fields[:band, inner]
        out_ref[place, half : 2 * half] = fields[band:, inner]
        out_ref[place, 2 * half :] = jnp.where(ends, fields[:band, other], roll(fields[band:, other], half // 2, 1))


def second_kernel(
    mean_ref, shift_ref, pair_ref,
    in_ref, source_ref, other_source_ref, diffusion_ref, reaction_ref, high_ref, low_ref,
    out_ref,
):
    mean, shift, place = mean_ref[0], shift_ref[0], pair_ref[0]
    table = (high_ref[...], low_ref[...])
    fields = product(split(in_ref[...]), table, 0, 0)
    half = fields.shape[0] // 3
    inner = pl.ds(pl.multiple_of(place * half, half), half)
    outer = pl.ds(pl.multiple_of((1 - place) * half, half), half)
    cells, others = diffusion_ref[inner, :], diffusion_ref[outer, :]
    reaction = reaction_ref[inner, :]
    row = lax.broadcasted_iota(jnp.int32, cells.shape, 0)
    top, bottom = row == 0, row == half - 1

    def after(values, beyond):
        return jnp.where(bottom, beyond, roll(values, -1, 0))

    def before(values, beyond):
        return jnp.where(top, beyond, roll(values, 1, 0))

    east = 0.5 * (cells + after(cells, others[0:1])) - mean
    west = 0.5 * (cells + before(cells, others[half - 1 : half])) - mean
    north = 0.5 * (cells + roll(cells, -1, 1)) - mean

    def linear(values, following, preceding):
        flux_y = north * (roll(values, -1, 1) - values)
        flux_x = east * (after(values, following) - values) - west * (values - before(values, preceding))
        return flux_x + flux_y - roll(flux_y, 1, 1) + shift * values

    state, adjoint = fields[:half], fields[half : 2 * half]
    beside = fields[2 * half :]
    middle = half // 2
    own_source, other_source = source_ref[inner, :], other_source_ref[...]
    state_source = jnp.where(place == 0, own_source, other_source)
    adjoint_source = jnp.where(place == 0, other_source, own_source)
    cube = reaction * state * state
    state_side = (
        state_source + linear(state, beside[0:1], beside[half - 1 : half]) - (cube * state + gamma_inv * adjoint)
    )
    adjoint_side = (
        adjoint_source
        + linear(adjoint, beside[middle : middle + 1], beside[middle - 1 : middle])
        - (3.0 * cube * adjoint - state)
    )
    sides = jnp.concatenate([state_side, adjoint_side], 0)
    out_ref[...] = product(table, split(sides), 1, 1)


def final_kernel(rows, total, scale, alpha_ref, in_ref, rate_ref, last_ref, high_ref, low_ref, out_ref, work_ref):
    table = (high_ref[...], low_ref[...])
    band = rows * total
    half = in_ref.shape[1] // 2
    joined = [
        jnp.concatenate([in_ref[:band, part], in_ref[band:, part]], 1)
        for part in (slice(0, half), slice(half, 2 * half))
    ]
    work_ref[...] = product(split(jnp.concatenate(joined, 0)), table, 1, 0)
    solve_steps(rows, total, scale, rate_ref[...], alpha_ref[0], last_ref, work_ref, None)
    out_ref[...] = product(split(work_ref[...]), table, 1, 0)


def close_kernel(in_ref, high_ref, low_ref, out_ref):
    out_ref[...] = product(split(in_ref[...]), (high_ref[...], low_ref[...]), 0, 0)


def call(kernel, scalars, arrays, out_shapes, scratch=()):
    spec_scalar = pl.BlockSpec(memory_space=pltpu.SMEM)
    spec_array = pl.BlockSpec(memory_space=pltpu.VMEM)
    return pl.pallas_call(
        kernel,
        out_shape=[jax.ShapeDtypeStruct(shape, jnp.float32) for shape in out_shapes],
        in_specs=[spec_scalar] * len(scalars) + [spec_array] * len(arrays),
        out_specs=[spec_array] * len(out_shapes),
        scratch_shapes=[pltpu.VMEM(shape, jnp.float32) for shape in scratch],
        compiler_params=pltpu.CompilerParams(vmem_limit_bytes=16 * 1024 * 1024),
    )(*scalars, *arrays)


def on_device(fields, forcing, diffusion, reaction, wrap_factor, mean_diffusion, spectral_shift):
    total = lax.axis_size("tm")
    place = lax.axis_index("pair")
    own, source = fields[0, 0], forcing[0, 0]
    grid_x, grid_y = own.shape
    half = grid_x // 2
    rows = grid_y // (2 * total)
    scale = 1.0 / (grid_x * grid_y)
    x_table, y_table = cas_table(grid_x), cas_table(grid_y)
    pair_flag = place.astype(jnp.int32).reshape(1)

    partner = lax.ppermute(own, "pair", [(0, 1), (1, 0)])
    wrap = lax.ppermute(own, AXES, [(total - 1, 0), (total, 2 * total - 1)])
    sent_source = lax.dynamic_slice_in_dim(source, (1 - place) * half, half, 0)
    other_source = lax.ppermute(sent_source, "pair", [(0, 1), (1, 0)])

    eigen_x = jnp.asarray((4.0 * np.sin(np.arange(grid_x) * (np.pi / grid_x)) ** 2).astype(np.float32))
    eigen_y = jnp.asarray((4.0 * np.sin(np.arange(grid_y) * (np.pi / grid_y)) ** 2).astype(np.float32))
    device = place * total + lax.axis_index("tm")
    eigen_y = lax.dynamic_slice_in_dim(eigen_y, device * rows, rows, 0)
    rate = 1.0 / (1.0 + spectral_shift + mean_diffusion * (eigen_y[:, None] + eigen_x[None, :]))

    def exchange(values):
        return lax.all_to_all(values, AXES, 0, 0, tiled=True)

    (sides,) = call(
        first_kernel,
        (mean_diffusion, spectral_shift, wrap_factor, pair_flag),
        (own, partner, wrap, source, diffusion, reaction, *y_table),
        [(grid_y, grid_x)],
    )
    halves, last = call(
        functools.partial(middle_kernel, rows, total, scale),
        (wrap_factor,),
        (exchange(sides), rate, *x_table),
        [(grid_y, 3 * half), (2 * rows, grid_x)],
        [(grid_y, grid_x)],
    )
    (sides,) = call(
        second_kernel,
        (mean_diffusion, spectral_shift, pair_flag),
        (exchange(halves), source, other_source, diffusion, reaction, *y_table),
        [(grid_y, grid_x)],
    )
    (wholes,) = call(
        functools.partial(final_kernel, rows, total, scale),
        (wrap_factor,),
        (exchange(sides), rate, last, *x_table),
        [(grid_y, grid_x)],
        [(grid_y, grid_x)],
    )
    (updated,) = call(close_kernel, (), (exchange(wholes), *y_table), [(grid_x, grid_y)])
    return updated[None, None]


def solution(mesh):
    in_specs = (P("pair", "tm", None, None), P("pair", "tm", None, None), P(), P(), P(), P(), P())
    out_specs = P("pair", "tm", None, None)
    return jax.shard_map(
        on_device, mesh=mesh, in_specs=in_specs, out_specs=out_specs, check_vma=False
    )
```

```python
import functools
import math

import jax
import jax.numpy as jnp
import ml_dtypes
import numpy as np
from jax import lax
from jax.experimental import pallas as pl
from jax.experimental.pallas import tpu as pltpu
from jax.sharding import PartitionSpec as P

gamma_inv = 0.5
AXES = ("pair", "tm")


def cas_table(length):
    places = np.arange(length)
    angles = (places[:, None] * places[None, :] % length) * (2.0 * np.pi / length)
    table = np.cos(angles) + np.sin(angles)
    high = table.astype(ml_dtypes.bfloat16)
    low = (table - high.astype(np.float64)).astype(ml_dtypes.bfloat16)
    return jnp.asarray(np.stack([high, low]))


def split(values):
    high = values.astype(jnp.bfloat16)
    return high, (values - high.astype(jnp.float32)).astype(jnp.bfloat16)


def product(left, right, left_dim, right_dim):
    dims = (((left_dim,), (right_dim,)), ((), ()))

    def one(a, b):
        return lax.dot_general(a, b, dims, preferred_element_type=jnp.float32)

    return one(left[0], right[0]) + (one(left[0], right[1]) + one(left[1], right[0]))


def roll(values, shift, axis):
    return pltpu.roll(values, shift % values.shape[axis], axis)


def coefficients(mean, shift, last):
    return jnp.where(last, 0.0, mean), jnp.where(last, -1.0, shift)


def own_kernel(
    total, rows,
    mean_ref, shift_ref, pair_ref, step_ref,
    own_ref, source_ref, diffusion_ref, reaction_ref, table_ref,
    side_ref, rate_ref,
):
    adjoint = pair_ref[0] == 1
    last = step_ref[0] == jnp.where(adjoint, 0, total - 1)
    mean, shift = coefficients(mean_ref[0], shift_ref[0], last)
    cells, own = diffusion_ref[...], own_ref[...]
    east = 0.5 * (cells + roll(cells, -1, 0)) - mean
    north = 0.5 * (cells + roll(cells, -1, 1)) - mean
    flux_x = east * (roll(own, -1, 0) - own)
    flux_y = north * (roll(own, -1, 1) - own)
    spread = flux_x - roll(flux_x, 1, 0) + flux_y - roll(flux_y, 1, 1)
    cube = jnp.where(adjoint, 0.0, 1.0) * (reaction_ref[...] * own * own * own)
    side_ref[...] = source_ref[...] + (spread + shift * own - cube)
    shape = rate_ref.shape
    band = (pair_ref[0] * total + step_ref[0]) * rows
    row_ids = band + lax.broadcasted_iota(jnp.int32, shape, 0)
    col_ids = lax.broadcasted_iota(jnp.int32, shape, 1)
    sine_rows = jnp.sin(row_ids.astype(jnp.float32) * (math.pi / own.shape[1]))
    sine_cols = jnp.sin(col_ids.astype(jnp.float32) * (math.pi / own.shape[0]))
    eigen = 4.0 * sine_rows * sine_rows + 4.0 * sine_cols * sine_cols
    rate_ref[...] = 1.0 / (1.0 + shift_ref[0] + mean_ref[0] * eigen)


def first_kernel(pair_ref, side_ref, own_ref, partner_ref, reaction_ref, table_ref, out_ref):
    partner = partner_ref[...]
    adjoint_part = 3.0 * reaction_ref[...] * partner * partner * own_ref[...] - partner
    side = side_ref[...] - jnp.where(pair_ref[0] == 1, adjoint_part, gamma_inv * partner)
    out_ref[...] = product(halves_of(table_ref), split(side), 1, 1)


def halves_of(table_ref):
    return table_ref[0], table_ref[1]


def step_places(group, total, rows):
    order = range(total) if group == 0 else range(total - 1, -1, -1)
    return [slice((group * total + step) * rows, (group * total + step + 1) * rows) for step in order]


def solve_steps(rows, total, rate, alpha, work_ref):
    power = rate
    for _ in range(total - 1):
        power = power * rate
    gain = alpha / (1.0 - alpha * power)
    for group in range(2):
        places = step_places(group, total, rows)
        value = jnp.zeros_like(rate)
        for place in places:
            value = rate * (value + work_ref[place, :])
        value = gain * value
        for place in places:
            value = rate * (value + work_ref[place, :])
            work_ref[place, :] = value


def middle_kernel(rows, total, scale, alpha_ref, in_ref, rate_ref, table_ref, out_ref, side_ref, last_ref, work_ref):
    table = halves_of(table_ref)
    sides = product(split(in_ref[...]), table, 1, 0) * scale
    side_ref[...] = sides
    work_ref[...] = sides
    solve_steps(rows, total, rate_ref[...], alpha_ref[0], work_ref)
    for group in range(2):
        last_ref[group * rows : (group + 1) * rows, :] = work_ref[step_places(group, total, rows)[-1], :]
    fields = product(split(work_ref[...]), table, 1, 0)
    band = rows * total
    half = fields.shape[1] // 2
    lane = lax.broadcasted_iota(jnp.int32, (band, half), 1)
    ends = (lane == 0) | (lane == half - 1)
    for side in range(2):
        inner = slice(side * half, (side + 1) * half)
        other = slice((1 - side) * half, (2 - side) * half)
        place = slice(side * band, (side + 1) * band)
        out_ref[place, :half] = fields[:band, inner]
        out_ref[place, half : 2 * half] = fields[band:, inner]
        out_ref[place, 2 * half :] = jnp.where(ends, fields[:band, other], roll(fields[band:, other], half // 2, 1))


def second_kernel(
    total,
    mean_ref, shift_ref, pair_ref, step_ref,
    in_ref, own_ref, partner_ref, diffusion_ref, reaction_ref, table_ref,
    out_ref,
):
    place, step = pair_ref[0], step_ref[0]
    table = halves_of(table_ref)
    solved = product(split(in_ref[...]), table, 0, 0)
    half = solved.shape[0] // 3
    middle = half // 2
    inner = pl.ds(pl.multiple_of(place * half, half), half)
    outer = pl.ds(pl.multiple_of((1 - place) * half, half), half)
    cells, others = diffusion_ref[inner, :], diffusion_ref[outer, :]
    reaction = reaction_ref[inner, :]
    row = lax.broadcasted_iota(jnp.int32, cells.shape, 0)
    top, bottom = row == 0, row == half - 1

    def after(values, beyond):
        return jnp.where(bottom, beyond, roll(values, -1, 0))

    def before(values, beyond):
        return jnp.where(top, beyond, roll(values, 1, 0))

    east = 0.5 * (cells + after(cells, others[0:1]))
    west = 0.5 * (cells + before(cells, others[half - 1 : half]))
    north = 0.5 * (cells + roll(cells, -1, 1))

    def linear(values, following, preceding, last):
        mean, shift = coefficients(mean_ref[0], shift_ref[0], last)
        flux_y = (north - mean) * (roll(values, -1, 1) - values)
        flux_x = (east - mean) * (after(values, following) - values)
        flux_x = flux_x - (west - mean) * (values - before(values, preceding))
        return flux_x + flux_y - roll(flux_y, 1, 1) + shift * values

    def change(group, first_row, last_step):
        own = place == group
        former_here = jnp.where(own, own_ref[inner, :], partner_ref[inner, :])
        former_there = jnp.where(own, own_ref[outer, :], partner_ref[outer, :])
        last = step == last_step
        taken = jnp.where(last, 0.0, 1.0)
        delta = solved[group * half : (group + 1) * half] - taken * former_here
        beside = solved[2 * half :]
        following = beside[first_row : first_row + 1] - taken * former_there[0:1]
        before_row = (first_row - 1) % half
        preceding = beside[before_row : before_row + 1] - taken * former_there[half - 1 : half]
        return former_here, delta, linear(delta, following, preceding, last)

    state, state_delta, state_side = change(0, 0, total - 1)
    adjoint, adjoint_delta, adjoint_side = change(1, middle, 0)
    new_state, new_adjoint = state + state_delta, adjoint + adjoint_delta
    square, new_square = state * state, new_state * new_state
    state_side = state_side - (reaction * (new_square * new_state - square * state) + gamma_inv * adjoint_delta)
    adjoint_side = adjoint_side - (3.0 * reaction * (new_square * new_adjoint - square * adjoint) - state_delta)
    sides = jnp.concatenate([state_side, adjoint_side], 0)
    out_ref[...] = product(table, split(sides), 1, 1)


def final_kernel(rows, total, scale, alpha_ref, in_ref, rate_ref, side_ref, last_ref, table_ref, out_ref, work_ref):
    table = halves_of(table_ref)
    band = rows * total
    half = in_ref.shape[1] // 2
    joined = [
        jnp.concatenate([in_ref[:band, part], in_ref[band:, part]], 1)
        for part in (slice(0, half), slice(half, 2 * half))
    ]
    work_ref[...] = product(split(jnp.concatenate(joined, 0)), table, 1, 0) * scale + side_ref[...]
    solve_steps(rows, total, rate_ref[...], alpha_ref[0], work_ref)
    for group in range(2):
        place = step_places(group, total, rows)[-1]
        work_ref[place, :] = work_ref[place, :] + last_ref[group * rows : (group + 1) * rows, :]
    out_ref[...] = product(split(work_ref[...]), table, 1, 0)


def close_kernel(total, pair_ref, step_ref, in_ref, own_ref, table_ref, out_ref):
    last = step_ref[0] == jnp.where(pair_ref[0] == 1, 0, total - 1)
    kept = jnp.where(last, 1.0, 0.0) * own_ref[...]
    out_ref[...] = kept + product(split(in_ref[...]), halves_of(table_ref), 0, 0)


def call(kernel, scalars, arrays, out_shapes, scratch=()):
    spec_scalar = pl.BlockSpec(memory_space=pltpu.SMEM)
    spec_array = pl.BlockSpec(memory_space=pltpu.VMEM)
    return pl.pallas_call(
        kernel,
        out_shape=[jax.ShapeDtypeStruct(shape, jnp.float32) for shape in out_shapes],
        in_specs=[spec_scalar] * len(scalars) + [spec_array] * len(arrays),
        out_specs=[spec_array] * len(out_shapes),
        scratch_shapes=[pltpu.VMEM(shape, jnp.float32) for shape in scratch],
        compiler_params=pltpu.CompilerParams(vmem_limit_bytes=16 * 1024 * 1024),
    )(*scalars, *arrays)


def on_device(fields, forcing, diffusion, reaction, wrap_factor, mean_diffusion, spectral_shift):
    total = lax.axis_size("tm")
    own, source = fields[0, 0], forcing[0, 0]
    grid_x, grid_y = own.shape
    half = grid_x // 2
    rows = grid_y // (2 * total)
    scale = 1.0 / (grid_x * grid_y)
    x_table, y_table = cas_table(grid_x), cas_table(grid_y)
    pair = lax.axis_index("pair").astype(jnp.int32).reshape(1)
    step = lax.axis_index("tm").astype(jnp.int32).reshape(1)
    grid, band = (grid_x, grid_y), (grid_y, grid_x)

    def exchange(values):
        return lax.all_to_all(values, AXES, 0, 0, tiled=True)

    partner = lax.ppermute(own, "pair", [(0, 1), (1, 0)])
    side, rate = call(
        functools.partial(own_kernel, total, rows),
        (mean_diffusion, spectral_shift, pair, step),
        (own, source, diffusion, reaction, y_table),
        [grid, (rows, grid_x)],
    )
    (sides,) = call(first_kernel, (pair,), (side, own, partner, reaction, y_table), [band])
    halves, kept_side, last = call(
        functools.partial(middle_kernel, rows, total, scale),
        (wrap_factor,),
        (exchange(sides), rate, x_table),
        [(grid_y, 3 * half), band, (2 * rows, grid_x)],
        [band],
    )
    (sides,) = call(
        functools.partial(second_kernel, total),
        (mean_diffusion, spectral_shift, pair, step),
        (exchange(halves), own, partner, diffusion, reaction, y_table),
        [band],
    )
    (wholes,) = call(
        functools.partial(final_kernel, rows, total, scale),
        (wrap_factor,),
        (exchange(sides), rate, kept_side, last, x_table),
        [band],
        [band],
    )
    (updated,) = call(
        functools.partial(close_kernel, total), (pair, step), (exchange(wholes), own, y_table), [grid]
    )
    return updated[None, None]


def solution(mesh):
    in_specs = (P("pair", "tm", None, None), P("pair", "tm", None, None), P(), P(), P(), P(), P())
    out_specs = P("pair", "tm", None, None)
    return jax.shard_map(
        on_device, mesh=mesh, in_specs=in_specs, out_specs=out_specs, check_vma=False
    )
```

```python
import functools
import math

import jax
import jax.numpy as jnp
import ml_dtypes
import numpy as np
from jax import lax
from jax.experimental import pallas as pl
from jax.experimental.pallas import tpu as pltpu
from jax.sharding import PartitionSpec as P

gamma_inv = 0.5
AXES = ("pair", "tm")


def cas_table(length):
    places = np.arange(length)
    angles = (places[:, None] * places[None, :] % length) * (2.0 * np.pi / length)
    table = np.cos(angles) + np.sin(angles)
    high = table.astype(ml_dtypes.bfloat16)
    low = (table - high.astype(np.float64)).astype(ml_dtypes.bfloat16)
    return jnp.asarray(np.stack([high, low]))


def split(values):
    high = values.astype(jnp.bfloat16)
    return high, (values - high.astype(jnp.float32)).astype(jnp.bfloat16)


def product(left, right, left_dim, right_dim):
    dims = (((left_dim,), (right_dim,)), ((), ()))

    def one(a, b):
        return lax.dot_general(a, b, dims, preferred_element_type=jnp.float32)

    return one(left[0], right[0]) + (one(left[0], right[1]) + one(left[1], right[0]))


def roll(values, shift, axis):
    return pltpu.roll(values, shift % values.shape[axis], axis)


def coefficients(mean, shift, last):
    return jnp.where(last, 0.0, mean), jnp.where(last, -1.0, shift)


def own_kernel(
    total, rows,
    mean_ref, shift_ref, alpha_ref, pair_ref, step_ref,
    own_ref, source_ref, diffusion_ref, reaction_ref, table_ref,
    side_ref, rate_ref, wrap_ref,
):
    adjoint = pair_ref[0] == 1
    last = step_ref[0] == jnp.where(adjoint, 0, total - 1)
    mean, shift = coefficients(mean_ref[0], shift_ref[0], last)
    cells, own = diffusion_ref[...], own_ref[...]
    east = 0.5 * (cells + roll(cells, -1, 0)) - mean
    north = 0.5 * (cells + roll(cells, -1, 1)) - mean
    flux_x = east * (roll(own, -1, 0) - own)
    flux_y = north * (roll(own, -1, 1) - own)
    spread = flux_x - roll(flux_x, 1, 0) + flux_y - roll(flux_y, 1, 1)
    cube = jnp.where(adjoint, 0.0, 1.0) * (reaction_ref[...] * own * own * own)
    side_ref[...] = source_ref[...] + (spread + shift * own - cube)
    shape = rate_ref.shape
    band = (pair_ref[0] * total + step_ref[0]) * rows
    row_ids = band + lax.broadcasted_iota(jnp.int32, shape, 0)
    col_ids = lax.broadcasted_iota(jnp.int32, shape, 1)
    sine_rows = jnp.sin(row_ids.astype(jnp.float32) * (math.pi / own.shape[1]))
    sine_cols = jnp.sin(col_ids.astype(jnp.float32) * (math.pi / own.shape[0]))
    eigen = 4.0 * sine_rows * sine_rows + 4.0 * sine_cols * sine_cols
    rate = 1.0 / (1.0 + shift_ref[0] + mean_ref[0] * eigen)
    rate_ref[...] = rate
    power = rate
    for _ in range(total - 1):
        power = power * rate
    wrap = alpha_ref[0] / (1.0 - alpha_ref[0] * power)
    for step in range(total):
        wrap = wrap * rate
        wrap_ref[step * rows : (step + 1) * rows, :] = wrap


def first_kernel(pair_ref, side_ref, own_ref, partner_ref, reaction_ref, table_ref, out_ref):
    partner = partner_ref[...]
    adjoint_part = 3.0 * reaction_ref[...] * partner * partner * own_ref[...] - partner
    side = side_ref[...] - jnp.where(pair_ref[0] == 1, adjoint_part, gamma_inv * partner)
    out_ref[...] = product(halves_of(table_ref), split(side), 1, 1)


def halves_of(table_ref):
    return table_ref[0], table_ref[1]


def step_places(group, total, rows):
    order = range(total) if group == 0 else range(total - 1, -1, -1)
    return [slice((group * total + step) * rows, (group * total + step + 1) * rows) for step in order]


def solve_steps(rows, total, rate, wrap_ref, work_ref):
    places = [step_places(group, total, rows) for group in range(2)]
    values = [jnp.zeros_like(rate)] * 2
    for step in range(total):
        for group in range(2):
            place = places[group][step]
            values[group] = rate * (values[group] + work_ref[place, :])
            work_ref[place, :] = values[group]
    for step in range(total):
        wrap = wrap_ref[step * rows : (step + 1) * rows, :]
        for group in range(2):
            place = places[group][step]
            work_ref[place, :] = work_ref[place, :] + wrap * values[group]


def middle_kernel(
    rows, total, scale, in_ref, rate_ref, wrap_ref, table_ref, out_ref, side_ref, last_ref, work_ref
):
    table = halves_of(table_ref)
    sides = product(split(in_ref[...]), table, 1, 0) * scale
    side_ref[...] = sides
    work_ref[...] = sides
    solve_steps(rows, total, rate_ref[...], wrap_ref, work_ref)
    for group in range(2):
        last_ref[group * rows : (group + 1) * rows, :] = work_ref[step_places(group, total, rows)[-1], :]
    fields = product(split(work_ref[...]), table, 1, 0)
    band = rows * total
    half = fields.shape[1] // 2
    lane = lax.broadcasted_iota(jnp.int32, (band, half), 1)
    ends = (lane == 0) | (lane == half - 1)
    for side in range(2):
        inner = slice(side * half, (side + 1) * half)
        other = slice((1 - side) * half, (2 - side) * half)
        place = slice(side * band, (side + 1) * band)
        out_ref[place, :half] = fields[:band, inner]
        out_ref[place, half : 2 * half] = fields[band:, inner]
        out_ref[place, 2 * half :] = jnp.where(ends, fields[:band, other], roll(fields[band:, other], half // 2, 1))


def second_kernel(
    total,
    mean_ref, shift_ref, pair_ref, step_ref,
    in_ref, own_ref, partner_ref, diffusion_ref, reaction_ref, table_ref,
    out_ref,
):
    place, step = pair_ref[0], step_ref[0]
    table = halves_of(table_ref)
    solved = product(split(in_ref[...]), table, 0, 0)
    half = solved.shape[0] // 3
    middle = half // 2
    inner = pl.ds(pl.multiple_of(place * half, half), half)
    outer = pl.ds(pl.multiple_of((1 - place) * half, half), half)
    cells, others = diffusion_ref[inner, :], diffusion_ref[outer, :]
    reaction = reaction_ref[inner, :]
    row = lax.broadcasted_iota(jnp.int32, cells.shape, 0)
    top, bottom = row == 0, row == half - 1

    def after(values, beyond):
        return jnp.where(bottom, beyond, roll(values, -1, 0))

    def before(values, beyond):
        return jnp.where(top, beyond, roll(values, 1, 0))

    east = 0.5 * (cells + after(cells, others[0:1]))
    west = 0.5 * (cells + before(cells, others[half - 1 : half]))
    north = 0.5 * (cells + roll(cells, -1, 1))

    def linear(values, following, preceding, last):
        mean, shift = coefficients(mean_ref[0], shift_ref[0], last)
        flux_y = (north - mean) * (roll(values, -1, 1) - values)
        flux_x = (east - mean) * (after(values, following) - values)
        flux_x = flux_x - (west - mean) * (values - before(values, preceding))
        return flux_x + flux_y - roll(flux_y, 1, 1) + shift * values

    def change(group, first_row, last_step):
        own = place == group
        former_here = jnp.where(own, own_ref[inner, :], partner_ref[inner, :])
        former_there = jnp.where(own, own_ref[outer, :], partner_ref[outer, :])
        last = step == last_step
        taken = jnp.where(last, 0.0, 1.0)
        delta = solved[group * half : (group + 1) * half] - taken * former_here
        beside = solved[2 * half :]
        following = beside[first_row : first_row + 1] - taken * former_there[0:1]
        before_row = (first_row - 1) % half
        preceding = beside[before_row : before_row + 1] - taken * former_there[half - 1 : half]
        return former_here, delta, linear(delta, following, preceding, last)

    state, state_delta, state_side = change(0, 0, total - 1)
    adjoint, adjoint_delta, adjoint_side = change(1, middle, 0)
    new_state, new_adjoint = state + state_delta, adjoint + adjoint_delta
    square, new_square = state * state, new_state * new_state
    state_side = state_side - (reaction * (new_square * new_state - square * state) + gamma_inv * adjoint_delta)
    adjoint_side = adjoint_side - (3.0 * reaction * (new_square * new_adjoint - square * adjoint) - state_delta)
    sides = jnp.concatenate([state_side, adjoint_side], 0)
    out_ref[...] = product(table, split(sides), 1, 1)


def final_kernel(
    rows, total, scale, in_ref, rate_ref, wrap_ref, side_ref, last_ref, table_ref, out_ref, work_ref
):
    table = halves_of(table_ref)
    band = rows * total
    half = in_ref.shape[1] // 2
    joined = [
        jnp.concatenate([in_ref[:band, part], in_ref[band:, part]], 1)
        for part in (slice(0, half), slice(half, 2 * half))
    ]
    work_ref[...] = product(split(jnp.concatenate(joined, 0)), table, 1, 0) * scale + side_ref[...]
    solve_steps(rows, total, rate_ref[...], wrap_ref, work_ref)
    for group in range(2):
        place = step_places(group, total, rows)[-1]
        work_ref[place, :] = work_ref[place, :] + last_ref[group * rows : (group + 1) * rows, :]
    out_ref[...] = product(split(work_ref[...]), table, 1, 0)


def close_kernel(total, pair_ref, step_ref, in_ref, own_ref, table_ref, out_ref):
    last = step_ref[0] == jnp.where(pair_ref[0] == 1, 0, total - 1)
    kept = jnp.where(last, 1.0, 0.0) * own_ref[...]
    out_ref[...] = kept + product(split(in_ref[...]), halves_of(table_ref), 0, 0)


def call(kernel, scalars, arrays, out_shapes, scratch=()):
    spec_scalar = pl.BlockSpec(memory_space=pltpu.SMEM)
    spec_array = pl.BlockSpec(memory_space=pltpu.VMEM)
    return pl.pallas_call(
        kernel,
        out_shape=[jax.ShapeDtypeStruct(shape, jnp.float32) for shape in out_shapes],
        in_specs=[spec_scalar] * len(scalars) + [spec_array] * len(arrays),
        out_specs=[spec_array] * len(out_shapes),
        scratch_shapes=[pltpu.VMEM(shape, jnp.float32) for shape in scratch],
        compiler_params=pltpu.CompilerParams(vmem_limit_bytes=16 * 1024 * 1024),
    )(*scalars, *arrays)


def on_device(fields, forcing, diffusion, reaction, wrap_factor, mean_diffusion, spectral_shift):
    total = lax.axis_size("tm")
    own, source = fields[0, 0], forcing[0, 0]
    grid_x, grid_y = own.shape
    half = grid_x // 2
    rows = grid_y // (2 * total)
    scale = 1.0 / (grid_x * grid_y)
    x_table, y_table = cas_table(grid_x), cas_table(grid_y)
    pair = lax.axis_index("pair").astype(jnp.int32).reshape(1)
    step = lax.axis_index("tm").astype(jnp.int32).reshape(1)
    grid, band = (grid_x, grid_y), (grid_y, grid_x)

    def exchange(values):
        return lax.all_to_all(values, AXES, 0, 0, tiled=True)

    partner = lax.ppermute(own, "pair", [(0, 1), (1, 0)])
    side, rate, wrap = call(
        functools.partial(own_kernel, total, rows),
        (mean_diffusion, spectral_shift, wrap_factor, pair, step),
        (own, source, diffusion, reaction, y_table),
        [grid, (rows, grid_x), (total * rows, grid_x)],
    )
    (sides,) = call(first_kernel, (pair,), (side, own, partner, reaction, y_table), [band])
    halves, kept_side, last = call(
        functools.partial(middle_kernel, rows, total, scale),
        (),
        (exchange(sides), rate, wrap, x_table),
        [(grid_y, 3 * half), band, (2 * rows, grid_x)],
        [band],
    )
    (sides,) = call(
        functools.partial(second_kernel, total),
        (mean_diffusion, spectral_shift, pair, step),
        (exchange(halves), own, partner, diffusion, reaction, y_table),
        [band],
    )
    (wholes,) = call(
        functools.partial(final_kernel, rows, total, scale),
        (),
        (exchange(sides), rate, wrap, kept_side, last, x_table),
        [band],
        [band],
    )
    (updated,) = call(
        functools.partial(close_kernel, total), (pair, step), (exchange(wholes), own, y_table), [grid]
    )
    return updated[None, None]


def solution(mesh):
    in_specs = (P("pair", "tm", None, None), P("pair", "tm", None, None), P(), P(), P(), P(), P())
    out_specs = P("pair", "tm", None, None)
    return jax.shard_map(
        on_device, mesh=mesh, in_specs=in_specs, out_specs=out_specs, check_vma=False
    )
```

```python
import functools
import math

import jax
import jax.numpy as jnp
import ml_dtypes
import numpy as np
from jax import lax
from jax.experimental import pallas as pl
from jax.experimental.pallas import tpu as pltpu
from jax.sharding import PartitionSpec as P

gamma_inv = 0.5
AXES = ("pair", "tm")


def cas_table(length):
    places = np.arange(length)
    angles = (places[:, None] * places[None, :] % length) * (2.0 * np.pi / length)
    table = np.cos(angles) + np.sin(angles)
    high = table.astype(ml_dtypes.bfloat16)
    low = (table - high.astype(np.float64)).astype(ml_dtypes.bfloat16)
    return jnp.asarray(np.stack([high, low]))


def split(values):
    high = values.astype(jnp.bfloat16)
    return high, (values - high.astype(jnp.float32)).astype(jnp.bfloat16)


def product(left, right, left_dim, right_dim):
    dims = (((left_dim,), (right_dim,)), ((), ()))

    def one(a, b):
        return lax.dot_general(a, b, dims, preferred_element_type=jnp.float32)

    return one(left[0], right[0]) + (one(left[0], right[1]) + one(left[1], right[0]))


def roll(values, shift, axis):
    return pltpu.roll(values, shift % values.shape[axis], axis)


def coefficients(mean, shift, last):
    return jnp.where(last, 0.0, mean), jnp.where(last, -1.0, shift)


def own_kernel(
    total, rows,
    mean_ref, shift_ref, alpha_ref, pair_ref, step_ref,
    own_ref, source_ref, diffusion_ref, reaction_ref, table_ref,
    side_ref, rate_ref, wrap_ref,
):
    adjoint = pair_ref[0] == 1
    last = step_ref[0] == jnp.where(adjoint, 0, total - 1)
    mean, shift = coefficients(mean_ref[0], shift_ref[0], last)
    cells, own = diffusion_ref[...], own_ref[...]
    east = 0.5 * (cells + roll(cells, -1, 0)) - mean
    north = 0.5 * (cells + roll(cells, -1, 1)) - mean
    flux_x = east * (roll(own, -1, 0) - own)
    flux_y = north * (roll(own, -1, 1) - own)
    spread = flux_x - roll(flux_x, 1, 0) + flux_y - roll(flux_y, 1, 1)
    cube = jnp.where(adjoint, 0.0, 1.0) * (reaction_ref[...] * own * own * own)
    side_ref[...] = source_ref[...] + (spread + shift * own - cube)
    shape = rate_ref.shape
    band = (pair_ref[0] * total + step_ref[0]) * rows
    row_ids = band + lax.broadcasted_iota(jnp.int32, shape, 0)
    col_ids = lax.broadcasted_iota(jnp.int32, shape, 1)
    sine_rows = jnp.sin(row_ids.astype(jnp.float32) * (math.pi / own.shape[1]))
    sine_cols = jnp.sin(col_ids.astype(jnp.float32) * (math.pi / own.shape[0]))
    eigen = 4.0 * sine_rows * sine_rows + 4.0 * sine_cols * sine_cols
    rate = 1.0 / (1.0 + shift_ref[0] + mean_ref[0] * eigen)
    rate_ref[...] = rate
    power = rate
    for _ in range(total - 1):
        power = power * rate
    wrap = alpha_ref[0] / (1.0 - alpha_ref[0] * power)
    for step in range(total):
        wrap = wrap * rate
        wrap_ref[step * rows : (step + 1) * rows, :] = wrap


def first_kernel(pair_ref, side_ref, own_ref, partner_ref, reaction_ref, table_ref, out_ref):
    partner = partner_ref[...]
    adjoint_part = 3.0 * reaction_ref[...] * partner * partner * own_ref[...] - partner
    side = side_ref[...] - jnp.where(pair_ref[0] == 1, adjoint_part, gamma_inv * partner)
    out_ref[...] = product(halves_of(table_ref), split(side), 1, 1)


def halves_of(table_ref):
    return table_ref[0], table_ref[1]


def step_places(group, total, rows):
    order = range(total) if group == 0 else range(total - 1, -1, -1)
    return [slice((group * total + step) * rows, (group * total + step + 1) * rows) for step in order]


def solve_steps(rows, total, rate, wrap_ref, work_ref):
    places = [step_places(group, total, rows) for group in range(2)]
    values = [jnp.zeros_like(rate)] * 2
    for step in range(total):
        for group in range(2):
            place = places[group][step]
            values[group] = rate * (values[group] + work_ref[place, :])
            work_ref[place, :] = values[group]
    for step in range(total):
        wrap = wrap_ref[step * rows : (step + 1) * rows, :]
        for group in range(2):
            place = places[group][step]
            work_ref[place, :] = work_ref[place, :] + wrap * values[group]


def middle_kernel(
    rows, total, scale, in_ref, rate_ref, wrap_ref, table_ref, out_ref, side_ref, last_ref, work_ref
):
    table = halves_of(table_ref)
    sides = product(split(in_ref[...]), table, 1, 0) * scale
    side_ref[...] = sides
    work_ref[...] = sides
    solve_steps(rows, total, rate_ref[...], wrap_ref, work_ref)
    for group in range(2):
        last_ref[group * rows : (group + 1) * rows, :] = work_ref[step_places(group, total, rows)[-1], :]
    fields = product(split(work_ref[...]), table, 1, 0)
    band = rows * total
    half = fields.shape[1] // 2
    block = 2 * rows + 1
    row = lax.broadcasted_iota(jnp.int32, (band, half), 0)
    lane = lax.broadcasted_iota(jnp.int32, (band, half), 1)
    for side in range(2):
        inner, outer = side * half, (1 - side) * half
        packed = jnp.zeros((band, half), jnp.float32)
        for group in range(2):
            for number, column in enumerate((outer, outer + half - 1)):
                values = fields[group * band : (group + 1) * band, column : column + 1]
                packed = jnp.where(lane == (2 * group + number) * rows + row % rows, values, packed)
        packed = packed.reshape(total, rows, half).sum(1)
        for step in range(total):
            start = (side * total + step) * block
            for group in range(2):
                place = slice((group * total + step) * rows, (group * total + step + 1) * rows)
                out_ref[start + group * rows : start + (group + 1) * rows, :] = fields[place, inner : inner + half]
            out_ref[start + 2 * rows : start + block, :] = packed[step : step + 1]


def second_kernel(
    total,
    mean_ref, shift_ref, pair_ref, step_ref,
    in_ref, own_ref, partner_ref, diffusion_ref, reaction_ref, table_ref,
    out_ref, work_ref,
):
    place, step = pair_ref[0], step_ref[0]
    table = halves_of(table_ref)
    grid_x, grid_y = own_ref.shape
    half = grid_x // 2
    rows = grid_y // (2 * total)
    block = 2 * rows + 1
    row = lax.broadcasted_iota(jnp.int32, (rows, half), 0)
    lane = lax.broadcasted_iota(jnp.int32, (rows, half), 1)
    diagonal = (lane % rows == row) & (lane < 4 * rows)
    for source in range(2 * total):
        start, band = source * block, slice(source * rows, (source + 1) * rows)
        for group in range(2):
            work_ref[band, group * half : (group + 1) * half] = in_ref[start + group * rows : start + (group + 1) * rows, :]
        work_ref[band, 2 * half :] = jnp.where(diagonal, in_ref[start + 2 * rows : start + block, :], 0.0)
    solved = product(split(work_ref[...]), table, 0, 0)
    beside = solved[2 * half : 2 * half + 4 * rows].reshape(4, rows, grid_y).sum(1)
    inner = pl.ds(pl.multiple_of(place * half, half), half)
    outer = pl.ds(pl.multiple_of((1 - place) * half, half), half)
    cells, others = diffusion_ref[inner, :], diffusion_ref[outer, :]
    reaction = reaction_ref[inner, :]
    row = lax.broadcasted_iota(jnp.int32, cells.shape, 0)
    top, bottom = row == 0, row == half - 1

    def after(values, beyond):
        return jnp.where(bottom, beyond, roll(values, -1, 0))

    def before(values, beyond):
        return jnp.where(top, beyond, roll(values, 1, 0))

    east = 0.5 * (cells + after(cells, others[0:1]))
    west = 0.5 * (cells + before(cells, others[half - 1 : half]))
    north = 0.5 * (cells + roll(cells, -1, 1))

    def linear(values, following, preceding, last):
        mean, shift = coefficients(mean_ref[0], shift_ref[0], last)
        flux_y = (north - mean) * (roll(values, -1, 1) - values)
        flux_x = (east - mean) * (after(values, following) - values)
        flux_x = flux_x - (west - mean) * (values - before(values, preceding))
        return flux_x + flux_y - roll(flux_y, 1, 1) + shift * values

    def change(group, last_step):
        own = place == group
        former_here = jnp.where(own, own_ref[inner, :], partner_ref[inner, :])
        former_there = jnp.where(own, own_ref[outer, :], partner_ref[outer, :])
        last = step == last_step
        taken = jnp.where(last, 0.0, 1.0)
        delta = solved[group * half : (group + 1) * half] - taken * former_here
        following = beside[2 * group : 2 * group + 1] - taken * former_there[0:1]
        preceding = beside[2 * group + 1 : 2 * group + 2] - taken * former_there[half - 1 : half]
        return former_here, delta, linear(delta, following, preceding, last)

    state, state_delta, state_side = change(0, total - 1)
    adjoint, adjoint_delta, adjoint_side = change(1, 0)
    new_state, new_adjoint = state + state_delta, adjoint + adjoint_delta
    square, new_square = state * state, new_state * new_state
    state_side = state_side - (reaction * (new_square * new_state - square * state) + gamma_inv * adjoint_delta)
    adjoint_side = adjoint_side - (3.0 * reaction * (new_square * new_adjoint - square * adjoint) - state_delta)
    sides = jnp.concatenate([state_side, adjoint_side], 0)
    out_ref[...] = product(table, split(sides), 1, 1)


def final_kernel(
    rows, total, scale, in_ref, rate_ref, wrap_ref, side_ref, last_ref, table_ref, out_ref, work_ref
):
    table = halves_of(table_ref)
    band = rows * total
    half = in_ref.shape[1] // 2
    joined = [
        jnp.concatenate([in_ref[:band, part], in_ref[band:, part]], 1)
        for part in (slice(0, half), slice(half, 2 * half))
    ]
    work_ref[...] = product(split(jnp.concatenate(joined, 0)), table, 1, 0) * scale + side_ref[...]
    solve_steps(rows, total, rate_ref[...], wrap_ref, work_ref)
    for group in range(2):
        place = step_places(group, total, rows)[-1]
        work_ref[place, :] = work_ref[place, :] + last_ref[group * rows : (group + 1) * rows, :]
    out_ref[...] = product(split(work_ref[...]), table, 1, 0)


def close_kernel(total, pair_ref, step_ref, in_ref, own_ref, table_ref, out_ref):
    last = step_ref[0] == jnp.where(pair_ref[0] == 1, 0, total - 1)
    kept = jnp.where(last, 1.0, 0.0) * own_ref[...]
    out_ref[...] = kept + product(split(in_ref[...]), halves_of(table_ref), 0, 0)


def call(kernel, scalars, arrays, out_shapes, scratch=()):
    spec_scalar = pl.BlockSpec(memory_space=pltpu.SMEM)
    spec_array = pl.BlockSpec(memory_space=pltpu.VMEM)
    return pl.pallas_call(
        kernel,
        out_shape=[jax.ShapeDtypeStruct(shape, jnp.float32) for shape in out_shapes],
        in_specs=[spec_scalar] * len(scalars) + [spec_array] * len(arrays),
        out_specs=[spec_array] * len(out_shapes),
        scratch_shapes=[pltpu.VMEM(shape, jnp.float32) for shape in scratch],
        compiler_params=pltpu.CompilerParams(vmem_limit_bytes=16 * 1024 * 1024),
    )(*scalars, *arrays)


def on_device(fields, forcing, diffusion, reaction, wrap_factor, mean_diffusion, spectral_shift):
    total = lax.axis_size("tm")
    own, source = fields[0, 0], forcing[0, 0]
    grid_x, grid_y = own.shape
    half = grid_x // 2
    rows = grid_y // (2 * total)
    scale = 1.0 / (grid_x * grid_y)
    x_table, y_table = cas_table(grid_x), cas_table(grid_y)
    pair = lax.axis_index("pair").astype(jnp.int32).reshape(1)
    step = lax.axis_index("tm").astype(jnp.int32).reshape(1)
    grid, band = (grid_x, grid_y), (grid_y, grid_x)

    def exchange(values):
        return lax.all_to_all(values, AXES, 0, 0, tiled=True)

    def exchange_blocks(values):
        blocks = values.reshape(2 * total, -1, 1, values.shape[1])
        return lax.all_to_all(blocks, AXES, 0, 0, tiled=True).reshape(values.shape)

    partner = lax.ppermute(own, "pair", [(0, 1), (1, 0)])
    side, rate, wrap = call(
        functools.partial(own_kernel, total, rows),
        (mean_diffusion, spectral_shift, wrap_factor, pair, step),
        (own, source, diffusion, reaction, y_table),
        [grid, (rows, grid_x), (total * rows, grid_x)],
    )
    (sides,) = call(first_kernel, (pair,), (side, own, partner, reaction, y_table), [band])
    halves, kept_side, last = call(
        functools.partial(middle_kernel, rows, total, scale),
        (),
        (exchange(sides), rate, wrap, x_table),
        [(2 * total * (2 * rows + 1), half), band, (2 * rows, grid_x)],
        [band],
    )
    (sides,) = call(
        functools.partial(second_kernel, total),
        (mean_diffusion, spectral_shift, pair, step),
        (exchange_blocks(halves), own, partner, diffusion, reaction, y_table),
        [band],
        [(grid_y, 3 * half)],
    )
    (wholes,) = call(
        functools.partial(final_kernel, rows, total, scale),
        (),
        (exchange(sides), rate, wrap, kept_side, last, x_table),
        [band],
        [band],
    )
    (updated,) = call(
        functools.partial(close_kernel, total), (pair, step), (exchange(wholes), own, y_table), [grid]
    )
    return updated[None, None]


def solution(mesh):
    in_specs = (P("pair", "tm", None, None), P("pair", "tm", None, None), P(), P(), P(), P(), P())
    out_specs = P("pair", "tm", None, None)
    return jax.shard_map(
        on_device, mesh=mesh, in_specs=in_specs, out_specs=out_specs, check_vma=False
    )
```

```python
import functools
import math

import jax
import jax.numpy as jnp
import ml_dtypes
import numpy as np
from jax import lax
from jax.experimental import pallas as pl
from jax.experimental.pallas import tpu as pltpu
from jax.sharding import PartitionSpec as P

ITERS = 2

gamma_inv = 0.5


def cas_table(length):
    places = np.arange(length)
    angles = (places[:, None] * places[None, :] % length) * (2.0 * np.pi / length)
    table = np.cos(angles) + np.sin(angles)
    high = table.astype(ml_dtypes.bfloat16)
    low = (table - high.astype(np.float64)).astype(ml_dtypes.bfloat16)
    return jnp.asarray(np.stack([high, low]))


def eigenvalues(length):
    return jnp.asarray((4.0 * np.sin(np.arange(length) * (np.pi / length)) ** 2).astype(np.float32))


def split(values):
    high = values.astype(jnp.bfloat16)
    return high, (values - high.astype(jnp.float32)).astype(jnp.bfloat16)


def parts(table_ref):
    return table_ref[0], table_ref[1]


def product(left, right):
    def one(a, b):
        return jnp.dot(a, b, preferred_element_type=jnp.float32)

    return one(left[0], right[0]) + (one(left[0], right[1]) + one(left[1], right[0]))


def roll(values, shift, axis):
    return pltpu.roll(values, shift % values.shape[axis], axis)


def own_kernel(mean_ref, shift_ref, adjoint_ref, last_ref, own_ref, source_ref, diffusion_ref, reaction_ref, out_ref):
    last = last_ref[0] == 1
    mean = jnp.where(last, 0.0, mean_ref[0])
    shift = jnp.where(last, -1.0, shift_ref[0])
    cells, own = diffusion_ref[...], own_ref[...]
    east = 0.5 * (cells + roll(cells, -1, 0)) - mean
    north = 0.5 * (cells + roll(cells, -1, 1)) - mean
    flux_x = east * (roll(own, -1, 0) - own)
    flux_y = north * (roll(own, -1, 1) - own)
    spread = flux_x - roll(flux_x, 1, 0) + flux_y - roll(flux_y, 1, 1)
    cube = jnp.where(adjoint_ref[0] == 1, 0.0, 1.0) * (reaction_ref[...] * own * own * own)
    out_ref[...] = source_ref[...] + (spread + shift * own - cube)


def forward_kernel(
    scale, adjoint_ref, core_ref, side_ref, own_ref, partner_ref, reaction_ref, x_ref, y_ref, keep_ref, send_ref, work_ref
):
    partner = partner_ref[...]
    adjoint_part = 3.0 * reaction_ref[...] * partner * partner * own_ref[...] - partner
    side = side_ref[...] - jnp.where(adjoint_ref[0] == 1, adjoint_part, gamma_inv * partner)
    rows = product(parts(x_ref), split(side))
    work_ref[...] = product(split(rows), parts(y_ref)) * scale
    half = keep_ref.shape[0]
    core = core_ref[0]
    keep_ref[...] = work_ref[pl.ds(pl.multiple_of(core * half, half), half), :]
    send_ref[...] = work_ref[pl.ds(pl.multiple_of((1 - core) * half, half), half), :]


def inverse_kernel(core_ref, last_ref, keep_ref, came_ref, own_ref, x_ref, y_ref, out_ref, work_ref):
    half = keep_ref.shape[0]
    core = core_ref[0]
    work_ref[pl.ds(pl.multiple_of(core * half, half), half), :] = keep_ref[...]
    work_ref[pl.ds(pl.multiple_of((1 - core) * half, half), half), :] = came_ref[...]
    rows = product(split(work_ref[...]), parts(y_ref))
    former = jnp.where(last_ref[0] == 1, 1.0, 0.0) * own_ref[...]
    out_ref[...] = former + product(parts(x_ref), split(rows))


def call(kernel, scalars, arrays, out_shapes, scratch=(), flops=0):
    spec_scalar = pl.BlockSpec(memory_space=pltpu.SMEM)
    spec_array = pl.BlockSpec(memory_space=pltpu.VMEM)
    return pl.pallas_call(
        kernel,
        out_shape=[jax.ShapeDtypeStruct(shape, jnp.float32) for shape in out_shapes],
        in_specs=[spec_scalar] * len(scalars) + [spec_array] * len(arrays),
        out_specs=[spec_array] * len(out_shapes),
        scratch_shapes=[pltpu.VMEM(shape, jnp.float32) for shape in scratch],
        compiler_params=pltpu.CompilerParams(vmem_limit_bytes=16 * 1024 * 1024),
    )(*scalars, *arrays)


def swap(values, axis, mask):
    return lax.ppermute(values, axis, [(i, i ^ mask) for i in range(lax.axis_size(axis))])


def power(base, exponent):
    result = None
    while exponent:
        if exponent & 1:
            result = base if result is None else result * base
        base, exponent = base * base, exponent >> 1
    return result


def solve_steps(kept, came, rate, alpha, place, total):
    odd = (place & 1) == 1
    first, second = jnp.where(odd, came, kept), jnp.where(odd, kept, came)
    carry = rate * (rate * first + second)
    levels = []
    bit, steps = 1, 2
    while steps < total:
        count = 4 if steps * 4 <= total else 2
        factor = power(rate, steps)
        powers = [jnp.ones_like(rate)]
        for _ in range(count - 1):
            powers.append(powers[-1] * factor)
        mine = (place >> bit) & (count - 1)
        alone = count == 2 and bit > 1
        masks = [number << bit for number in range(1, count)]
        if alone:
            masks = [(1 << bit) | (1 << (bit - 1))]
        pieces = [carry] + [swap(carry, "tm", mask) for mask in masks]
        whole, before = jnp.zeros_like(rate), jnp.zeros_like(rate)
        for number, piece in enumerate(pieces):
            index = mine ^ number
            weight, ahead = powers[count - 1], jnp.zeros_like(rate)
            for choice in range(1, count):
                weight = jnp.where(index == choice, powers[count - 1 - choice], weight)
            for gap in range(1, count):
                ahead = jnp.where(mine - index == gap, powers[gap - 1], ahead)
            whole = whole + weight * piece
            before = before + ahead * piece
        reach = powers[0]
        for choice in range(1, count):
            reach = jnp.where(mine == choice, powers[choice], reach)
        levels.append((reach, before))
        carry, bit, steps = whole, bit + count.bit_length() - 1, steps * count
    entering = alpha * carry / (1.0 - alpha * power(rate, total))
    for reach, before in reversed(levels):
        entering = reach * entering + before
    first = rate * (entering + first)
    second = rate * (first + second)
    return jnp.where(odd, second, first), jnp.where(odd, first, second)


def on_device(fields, forcing, diffusion, reaction, wrap_factor, mean_diffusion, spectral_shift):
    total = lax.axis_size("tm")
    own, source = fields[0, 0], forcing[0, 0]
    grid_x, grid_y = own.shape
    half = grid_x // 2
    scale = 1.0 / (grid_x * grid_y)
    x_table, y_table = cas_table(grid_x), cas_table(grid_y)
    group, step = lax.axis_index("pair"), lax.axis_index("tm")
    place = jnp.where(group == 1, total - 1 - step, step)
    core = step & 1

    def scalar(value):
        return value.astype(jnp.int32).reshape(1)

    adjoint, last, side_of = scalar(group), scalar(place == total - 1), scalar(core)
    eigen_x = lax.dynamic_slice_in_dim(eigenvalues(grid_x), core * half, half, 0)
    rate = 1.0 / (1.0 + spectral_shift + mean_diffusion * (eigen_x[:, None] + eigenvalues(grid_y)[None, :]))

    for _ in range(ITERS):
        partner = swap(own, "pair", 1)
        (side,) = call(
            own_kernel,
            (mean_diffusion, spectral_shift, adjoint, last),
            (own, source, diffusion, reaction),
            [own.shape],
        )
        keep, send = call(
            functools.partial(forward_kernel, scale),
            (adjoint, side_of),
            (side, own, partner, reaction, x_table, y_table),
            [(half, grid_y)] * 2,
            [own.shape],
        )
        keep, send = solve_steps(keep, swap(send, "tm", 1), rate, wrap_factor, place, total)
        (own,) = call(
            inverse_kernel,
            (side_of, last),
            (keep, swap(send, "tm", 1), own, x_table, y_table),
            [own.shape],
            [own.shape],
        )
    return own[None, None]


def solution(mesh):
    in_specs = (P("pair", "tm", None, None), P("pair", "tm", None, None), P(), P(), P(), P(), P())
    out_specs = P("pair", "tm", None, None)
    return jax.shard_map(
        on_device, mesh=mesh, in_specs=in_specs, out_specs=out_specs, check_vma=False
    )
```

```python
import functools
import math

import jax
import jax.numpy as jnp
import ml_dtypes
import numpy as np
from jax import lax
from jax.experimental import pallas as pl
from jax.experimental.pallas import tpu as pltpu
from jax.sharding import PartitionSpec as P

ITERS = 2

gamma_inv = 0.5


def cas_table(length):
    places = np.arange(length)
    angles = (places[:, None] * places[None, :] % length) * (2.0 * np.pi / length)
    table = np.cos(angles) + np.sin(angles)
    high = table.astype(ml_dtypes.bfloat16)
    low = (table - high.astype(np.float64)).astype(ml_dtypes.bfloat16)
    return jnp.asarray(np.stack([high, low]))


def eigenvalues(length):
    return jnp.asarray((4.0 * np.sin(np.arange(length) * (np.pi / length)) ** 2).astype(np.float32))


def split(values):
    high = values.astype(jnp.bfloat16)
    return high, (values - high.astype(jnp.float32)).astype(jnp.bfloat16)


def parts(table_ref):
    return table_ref[0], table_ref[1]


def product(left, right):
    def one(a, b):
        return jnp.dot(a, b, preferred_element_type=jnp.float32)

    return one(left[0], right[0]) + (one(left[0], right[1]) + one(left[1], right[0]))


def roll(values, shift, axis):
    return pltpu.roll(values, shift % values.shape[axis], axis)


def own_kernel(mean_ref, shift_ref, adjoint_ref, last_ref, own_ref, source_ref, diffusion_ref, reaction_ref, out_ref):
    last = last_ref[0] == 1
    mean = jnp.where(last, 0.0, mean_ref[0])
    shift = jnp.where(last, -1.0, shift_ref[0])
    cells, own = diffusion_ref[...], own_ref[...]
    east = 0.5 * (cells + roll(cells, -1, 0)) - mean
    north = 0.5 * (cells + roll(cells, -1, 1)) - mean
    flux_x = east * (roll(own, -1, 0) - own)
    flux_y = north * (roll(own, -1, 1) - own)
    spread = flux_x - roll(flux_x, 1, 0) + flux_y - roll(flux_y, 1, 1)
    cube = jnp.where(adjoint_ref[0] == 1, 0.0, 1.0) * (reaction_ref[...] * own * own * own)
    out_ref[...] = source_ref[...] + (spread + shift * own - cube)


def gather_halves(core, work_ref, kept_ref, came_ref):
    half = kept_ref.shape[0]
    work_ref[pl.ds(pl.multiple_of(core * half, half), half), :] = kept_ref[...]
    work_ref[pl.ds(pl.multiple_of((1 - core) * half, half), half), :] = came_ref[...]
    return split(work_ref[...])


def forward(scale, adjoint, core, side, own, partner, reaction, x_table, y_table, keep_ref, send_ref, work_ref):
    adjoint_part = 3.0 * reaction * partner * partner * own - partner
    side = side - jnp.where(adjoint, adjoint_part, gamma_inv * partner)
    rows = product(x_table, split(side))
    work_ref[...] = product(split(rows), y_table) * scale
    half = keep_ref.shape[0]
    keep_ref[...] = work_ref[pl.ds(pl.multiple_of(core * half, half), half), :]
    send_ref[...] = work_ref[pl.ds(pl.multiple_of((1 - core) * half, half), half), :]


def first_kernel(
    scale, adjoint_ref, core_ref, side_ref, own_ref, partner_ref, reaction_ref, x_ref, y_ref, keep_ref, send_ref, work_ref
):
    forward(
        scale, adjoint_ref[0] == 1, core_ref[0], side_ref[...], own_ref[...], partner_ref[...], reaction_ref[...],
        parts(x_ref), parts(y_ref), keep_ref, send_ref, work_ref,
    )


def later_kernel(
    scale, adjoint_ref, core_ref, partner_last_ref,
    side_ref, own_ref, kept_ref, came_ref, former_ref, reaction_ref, x_ref, y_ref,
    keep_ref, send_ref, *refs,
):
    x_table, y_table = parts(x_ref), parts(y_ref)
    work_ref = refs[-1]
    rows = product(gather_halves(core_ref[0], work_ref, kept_ref, came_ref), y_table)
    former = jnp.where(partner_last_ref[0] == 1, 1.0, 0.0) * former_ref[...]
    partner = former + product(x_table, split(rows))
    if len(refs) > 1:
        refs[0][...] = partner
    forward(
        scale, adjoint_ref[0] == 1, core_ref[0], side_ref[...], own_ref[...], partner, reaction_ref[...],
        x_table, y_table, keep_ref, send_ref, work_ref,
    )


def inverse_kernel(core_ref, last_ref, kept_ref, came_ref, own_ref, x_ref, y_ref, out_ref, work_ref):
    rows = product(gather_halves(core_ref[0], work_ref, kept_ref, came_ref), parts(y_ref))
    former = jnp.where(last_ref[0] == 1, 1.0, 0.0) * own_ref[...]
    out_ref[...] = former + product(parts(x_ref), split(rows))


def steps_kernel(odd_ref, entering_ref, kept_ref, came_ref, rate_ref, new_ref, sent_ref):
    odd = odd_ref[0] == 1
    kept, came, rate = kept_ref[...], came_ref[...], rate_ref[...]
    first = rate * (entering_ref[...] + jnp.where(odd, came, kept))
    second = rate * (first + jnp.where(odd, kept, came))
    new_ref[...] = jnp.where(odd, second, first)
    sent_ref[...] = jnp.where(odd, first, second)


def call(kernel, scalars, arrays, out_shapes, scratch=(), flops=0):
    spec_scalar = pl.BlockSpec(memory_space=pltpu.SMEM)
    spec_array = pl.BlockSpec(memory_space=pltpu.VMEM)
    return pl.pallas_call(
        kernel,
        out_shape=[jax.ShapeDtypeStruct(shape, jnp.float32) for shape in out_shapes],
        in_specs=[spec_scalar] * len(scalars) + [spec_array] * len(arrays),
        out_specs=[spec_array] * len(out_shapes),
        scratch_shapes=[pltpu.VMEM(shape, jnp.float32) for shape in scratch],
        compiler_params=pltpu.CompilerParams(vmem_limit_bytes=16 * 1024 * 1024),
    )(*scalars, *arrays)


def swap(values, axis, mask):
    return lax.ppermute(values, axis, [(i, i ^ mask) for i in range(lax.axis_size(axis))])


def power(base, exponent):
    result = None
    while exponent:
        if exponent & 1:
            result = base if result is None else result * base
        base, exponent = base * base, exponent >> 1
    return result


def pick(options, index):
    result = options[0]
    for number in range(1, len(options)):
        result = jnp.where(index == number, options[number], result)
    return result


def scan_factors(rate, alpha, place, total):
    none = jnp.zeros_like(rate)
    pair = (pick([rate * rate, rate], place & 1), pick([rate, rate * rate], place & 1))
    all_masks, levels, reach = [], [], None
    bit, steps = 1, 2
    while steps < total:
        count = 4 if steps * 4 <= total else 2
        masks = [number << bit for number in range(1, count)]
        if count == 2 and bit > 1:
            masks = [(1 << bit) | (1 << (bit - 1))]
        factor = power(rate, steps)
        powers = [jnp.ones_like(rate)]
        for _ in range(count - 1):
            powers.append(powers[-1] * factor)
        mine = (place >> bit) & (count - 1)
        join = [pick(powers[::-1], mine ^ number) for number in range(count)]
        enter = [pick([none] + powers, jnp.maximum(mine - (mine ^ number), 0)) for number in range(count)]
        through = pick(powers, mine)
        bit, steps = bit + count.bit_length() - 1, steps * count
        if steps == total:
            round_trip = alpha / (1.0 - alpha * power(rate, total)) * through
            enter = [round_trip * one + two for one, two in zip(join, enter)]
        if reach is not None:
            enter = [reach * one for one in enter]
        reach = through if reach is None else reach * through
        all_masks.append(masks)
        levels.append((join, enter))
    pair, levels = lax.optimization_barrier((pair, levels))
    return pair, [(masks, *level) for masks, level in zip(all_masks, levels)]


def carry_in(kept, came, pair, levels, share):
    others = [swap(kept, "pair", 1), swap(came, "pair", 1)] if share else [None, None]
    carry = pair[0] * kept + pair[1] * came
    entering = jnp.zeros_like(carry)
    for masks, join, enter in levels[:-1]:
        pieces = [carry] + [swap(carry, "tm", mask) for mask in masks]
        carry = sum(one * piece for one, piece in zip(join, pieces))
        entering = entering + sum(one * piece for one, piece in zip(enter, pieces))
    carry, others[0] = lax.optimization_barrier((carry, others[0]))
    masks, _, enter = levels[-1]
    entering = lax.optimization_barrier(entering + enter[0] * carry)
    entering = entering + sum(one * swap(carry, "tm", mask) for one, mask in zip(enter[1:], masks))
    return lax.optimization_barrier((entering, others))


def on_device(fields, forcing, diffusion, reaction, wrap_factor, mean_diffusion, spectral_shift):
    total = lax.axis_size("tm")
    own, source = fields[0, 0], forcing[0, 0]
    grid_x, grid_y = own.shape
    half = grid_x // 2
    scale = 1.0 / (grid_x * grid_y)
    tables = cas_table(grid_x), cas_table(grid_y)
    group, step = lax.axis_index("pair"), lax.axis_index("tm")
    place = jnp.where(group == 1, total - 1 - step, step)
    other_place = total - 1 - place
    core = step & 1

    def scalar(value):
        return value.astype(jnp.int32).reshape(1)

    adjoint, side_of = scalar(group), scalar(core)
    odd, other_odd = scalar(place & 1), scalar(other_place & 1)
    last, other_last = scalar(place == total - 1), scalar(other_place == total - 1)
    eigen_x = lax.dynamic_slice_in_dim(eigenvalues(grid_x), core * half, half, 0)
    rate = 1.0 / (1.0 + spectral_shift + mean_diffusion * (eigen_x[:, None] + eigenvalues(grid_y)[None, :]))
    pair, levels = scan_factors(rate, wrap_factor, place, total)

    def own_side(own):
        (side,) = call(
            own_kernel,
            (mean_diffusion, spectral_shift, adjoint, last),
            (own, source, diffusion, reaction),
            [own.shape],
        )
        return side

    def both_steps(odd, entering, kept, came):
        return call(steps_kernel, (odd,), (entering, kept, came, rate), [kept.shape] * 2)

    partner = [swap(own, "pair", 1)]
    side = own_side(own)
    for iteration in range(ITERS):
        more = iteration + 1 < ITERS
        if iteration == 0:
            kept, sent = call(
                functools.partial(first_kernel, scale),
                (adjoint, side_of),
                (side, own, *partner, reaction, *tables),
                [(half, grid_y)] * 2,
                [own.shape],
            )
        else:
            kept, sent, *partner = call(
                functools.partial(later_kernel, scale),
                (adjoint, side_of, other_last),
                (side, own, other_kept, other_came, *partner, reaction, *tables),
                [(half, grid_y)] * 2 + [own.shape] * more,
                [own.shape],
            )
        came = swap(sent, "tm", 1)
        entering, other_sides = carry_in(kept, came, pair, levels, more)
        new, sent = both_steps(odd, entering, kept, came)
        if more:
            other_entering = swap(entering, "pair", 1)
        (own,) = call(
            inverse_kernel,
            (side_of, last),
            (new, swap(sent, "tm", 1), own, *tables),
            [own.shape],
            [own.shape],
        )
        if more:
            side = own_side(own)
            other_entering, side = lax.optimization_barrier((other_entering, side))
            other_kept, other_sent = both_steps(other_odd, other_entering, *other_sides)
            other_came = swap(other_sent, "tm", 1)
    return own[None, None]


def solution(mesh):
    in_specs = (P("pair", "tm", None, None), P("pair", "tm", None, None), P(), P(), P(), P(), P())
    out_specs = P("pair", "tm", None, None)
    return jax.shard_map(
        on_device, mesh=mesh, in_specs=in_specs, out_specs=out_specs, check_vma=False
    )
```

```python
import functools
import math

import jax
import jax.numpy as jnp
import ml_dtypes
import numpy as np
from jax import lax
from jax.experimental import pallas as pl
from jax.experimental.pallas import tpu as pltpu
from jax.sharding import PartitionSpec as P

ITERS = 2

gamma_inv = 0.5


def cas_table(length):
    places = np.arange(length)
    angles = (places[:, None] * places[None, :] % length) * (2.0 * np.pi / length)
    table = np.cos(angles) + np.sin(angles)
    high = table.astype(ml_dtypes.bfloat16)
    low = (table - high.astype(np.float64)).astype(ml_dtypes.bfloat16)
    return jnp.asarray(np.stack([high, low]))


def eigenvalues(length):
    return jnp.asarray((4.0 * np.sin(np.arange(length) * (np.pi / length)) ** 2).astype(np.float32))


def split(values):
    high = values.astype(jnp.bfloat16)
    return high, (values - high.astype(jnp.float32)).astype(jnp.bfloat16)


def parts(table_ref):
    return table_ref[0], table_ref[1]


def product(left, right):
    def one(a, b):
        return jnp.dot(a, b, preferred_element_type=jnp.float32)

    return one(left[0], right[0]) + (one(left[0], right[1]) + one(left[1], right[0]))


def roll(values, shift, axis):
    return pltpu.roll(values, shift % values.shape[axis], axis)


def own_kernel(mean_ref, shift_ref, adjoint_ref, last_ref, own_ref, source_ref, diffusion_ref, reaction_ref, out_ref):
    last = last_ref[0] == 1
    mean = jnp.where(last, 0.0, mean_ref[0])
    shift = jnp.where(last, -1.0, shift_ref[0])
    cells, own = diffusion_ref[...], own_ref[...]
    east = 0.5 * (cells + roll(cells, -1, 0)) - mean
    north = 0.5 * (cells + roll(cells, -1, 1)) - mean
    flux_x = east * (roll(own, -1, 0) - own)
    flux_y = north * (roll(own, -1, 1) - own)
    spread = flux_x - roll(flux_x, 1, 0) + flux_y - roll(flux_y, 1, 1)
    cube = jnp.where(adjoint_ref[0] == 1, 0.0, 1.0) * (reaction_ref[...] * own * own * own)
    out_ref[...] = source_ref[...] + (spread + shift * own - cube)


def gather_halves(core, work_ref, kept_ref, came_ref):
    half = kept_ref.shape[0]
    work_ref[pl.ds(pl.multiple_of(core * half, half), half), :] = kept_ref[...]
    work_ref[pl.ds(pl.multiple_of((1 - core) * half, half), half), :] = came_ref[...]
    return split(work_ref[...])


def row_halves(count):
    return slice(0, count // 2), slice(count // 2, count)


def both_sides(x_ref, middle, y_table, place):
    return product(split(product((x_ref[0, place], x_ref[1, place]), middle)), y_table)


def forward(scale, adjoint, core, side, own, partner, reaction, x_ref, y_ref, keep_ref, send_ref, work_ref):
    adjoint_part = 3.0 * reaction * partner * partner * own - partner
    side = split(side - jnp.where(adjoint, adjoint_part, gamma_inv * partner))
    for place in row_halves(work_ref.shape[0]):
        work_ref[place, :] = both_sides(x_ref, side, parts(y_ref), place) * scale
    half = keep_ref.shape[0]
    keep_ref[...] = work_ref[pl.ds(pl.multiple_of(core * half, half), half), :]
    send_ref[...] = work_ref[pl.ds(pl.multiple_of((1 - core) * half, half), half), :]


def first_kernel(
    scale, adjoint_ref, core_ref, side_ref, own_ref, partner_ref, reaction_ref, x_ref, y_ref, keep_ref, send_ref, work_ref
):
    forward(
        scale, adjoint_ref[0] == 1, core_ref[0], side_ref[...], own_ref[...], partner_ref[...], reaction_ref[...],
        x_ref, y_ref, keep_ref, send_ref, work_ref,
    )


def later_kernel(
    scale, adjoint_ref, core_ref, partner_last_ref,
    side_ref, own_ref, kept_ref, came_ref, former_ref, reaction_ref, x_ref, y_ref,
    keep_ref, send_ref, *refs,
):
    work_ref = refs[-1]
    modes = gather_halves(core_ref[0], work_ref, kept_ref, came_ref)
    former = jnp.where(partner_last_ref[0] == 1, 1.0, 0.0) * former_ref[...]
    partner = former + both_sides(x_ref, modes, parts(y_ref), slice(None))
    if len(refs) > 1:
        refs[0][...] = partner
    forward(
        scale, adjoint_ref[0] == 1, core_ref[0], side_ref[...], own_ref[...], partner, reaction_ref[...],
        x_ref, y_ref, keep_ref, send_ref, work_ref,
    )


def inverse_kernel(core_ref, last_ref, kept_ref, came_ref, own_ref, x_ref, y_ref, out_ref, work_ref):
    modes = gather_halves(core_ref[0], work_ref, kept_ref, came_ref)
    former = jnp.where(last_ref[0] == 1, 1.0, 0.0)
    for place in row_halves(work_ref.shape[0]):
        out_ref[place, :] = former * own_ref[place, :] + both_sides(x_ref, modes, parts(y_ref), place)


def steps_kernel(odd_ref, entering_ref, kept_ref, came_ref, rate_ref, new_ref, sent_ref):
    odd = odd_ref[0] == 1
    kept, came, rate = kept_ref[...], came_ref[...], rate_ref[...]
    first = rate * (entering_ref[...] + jnp.where(odd, came, kept))
    second = rate * (first + jnp.where(odd, kept, came))
    new_ref[...] = jnp.where(odd, second, first)
    sent_ref[...] = jnp.where(odd, first, second)


def call(kernel, scalars, arrays, out_shapes, scratch=(), flops=0):
    spec_scalar = pl.BlockSpec(memory_space=pltpu.SMEM)
    spec_array = pl.BlockSpec(memory_space=pltpu.VMEM)
    return pl.pallas_call(
        kernel,
        out_shape=[jax.ShapeDtypeStruct(shape, jnp.float32) for shape in out_shapes],
        in_specs=[spec_scalar] * len(scalars) + [spec_array] * len(arrays),
        out_specs=[spec_array] * len(out_shapes),
        scratch_shapes=[pltpu.VMEM(shape, jnp.float32) for shape in scratch],
        compiler_params=pltpu.CompilerParams(vmem_limit_bytes=16 * 1024 * 1024),
    )(*scalars, *arrays)


def swap(values, axis, mask):
    return lax.ppermute(values, axis, [(i, i ^ mask) for i in range(lax.axis_size(axis))])


def power(base, exponent):
    result = None
    while exponent:
        if exponent & 1:
            result = base if result is None else result * base
        base, exponent = base * base, exponent >> 1
    return result


def pick(options, index):
    result = options[0]
    for number in range(1, len(options)):
        result = jnp.where(index == number, options[number], result)
    return result


def scan_factors(rate, alpha, place, total):
    none = jnp.zeros_like(rate)
    pair = (pick([rate * rate, rate], place & 1), pick([rate, rate * rate], place & 1))
    all_masks, levels, reach = [], [], None
    bit, steps = 1, 2
    while steps < total:
        count = 4 if steps * 4 <= total else 2
        numbers = [2, 3, 1] if count == 4 else [1]
        masks = [number << bit for number in numbers]
        if count == 2 and bit > 1:
            masks = [(1 << bit) | (1 << (bit - 1))]
        factor = power(rate, steps)
        powers = [jnp.ones_like(rate)]
        for _ in range(count - 1):
            powers.append(powers[-1] * factor)
        mine = (place >> bit) & (count - 1)
        join = [pick(powers[::-1], mine ^ number) for number in [0] + numbers]
        enter = [pick([none] + powers, jnp.maximum(mine - (mine ^ number), 0)) for number in [0] + numbers]
        through = pick(powers, mine)
        bit, steps = bit + count.bit_length() - 1, steps * count
        if steps == total:
            round_trip = alpha / (1.0 - alpha * power(rate, total)) * through
            enter = [round_trip * one + two for one, two in zip(join, enter)]
        if reach is not None:
            enter = [reach * one for one in enter]
        reach = through if reach is None else reach * through
        all_masks.append(masks)
        levels.append((join, enter))
    pair, levels = lax.optimization_barrier((pair, levels))
    return pair, [(masks, *level) for masks, level in zip(all_masks, levels)]


def carry_in(kept, came, pair, levels, share):
    others = [swap(kept, "pair", 1), swap(came, "pair", 1)] if share else [None, None]
    carry = pair[0] * kept + pair[1] * came
    entering = jnp.zeros_like(carry)
    for masks, join, enter in levels[:-1]:
        pieces = [carry] + [swap(carry, "tm", mask) for mask in masks]
        carry = sum(one * piece for one, piece in zip(join, pieces))
        entering = entering + sum(one * piece for one, piece in zip(enter, pieces))
    carry, others[0] = lax.optimization_barrier((carry, others[0]))
    masks, _, enter = levels[-1]
    entering = lax.optimization_barrier(entering + enter[0] * carry)
    entering = entering + sum(one * swap(carry, "tm", mask) for one, mask in zip(enter[1:], masks))
    return lax.optimization_barrier((entering, others))


def on_device(fields, forcing, diffusion, reaction, wrap_factor, mean_diffusion, spectral_shift):
    total = lax.axis_size("tm")
    own, source = fields[0, 0], forcing[0, 0]
    grid_x, grid_y = own.shape
    half = grid_x // 2
    scale = 1.0 / (grid_x * grid_y)
    tables = cas_table(grid_x), cas_table(grid_y)
    group, step = lax.axis_index("pair"), lax.axis_index("tm")
    place = jnp.where(group == 1, total - 1 - step, step)
    other_place = total - 1 - place
    core = step & 1

    def scalar(value):
        return value.astype(jnp.int32).reshape(1)

    adjoint, side_of = scalar(group), scalar(core)
    odd, other_odd = scalar(place & 1), scalar(other_place & 1)
    last, other_last = scalar(place == total - 1), scalar(other_place == total - 1)
    eigen_x = lax.dynamic_slice_in_dim(eigenvalues(grid_x), core * half, half, 0)
    rate = 1.0 / (1.0 + spectral_shift + mean_diffusion * (eigen_x[:, None] + eigenvalues(grid_y)[None, :]))
    pair, levels = scan_factors(rate, wrap_factor, place, total)

    def own_side(own):
        (side,) = call(
            own_kernel,
            (mean_diffusion, spectral_shift, adjoint, last),
            (own, source, diffusion, reaction),
            [own.shape],
        )
        return side

    def both_steps(odd, entering, kept, came):
        return call(steps_kernel, (odd,), (entering, kept, came, rate), [kept.shape] * 2)

    partner = [swap(own, "pair", 1)]
    side = own_side(own)
    for iteration in range(ITERS):
        more = iteration + 1 < ITERS
        if iteration == 0:
            kept, sent = call(
                functools.partial(first_kernel, scale),
                (adjoint, side_of),
                (side, own, *partner, reaction, *tables),
                [(half, grid_y)] * 2,
                [own.shape],
            )
        else:
            kept, sent, *partner = call(
                functools.partial(later_kernel, scale),
                (adjoint, side_of, other_last),
                (side, own, other_kept, other_came, *partner, reaction, *tables),
                [(half, grid_y)] * 2 + [own.shape] * more,
                [own.shape],
            )
        came = swap(sent, "tm", 1)
        entering, other_sides = carry_in(kept, came, pair, levels, more)
        new, sent = both_steps(odd, entering, kept, came)
        if more:
            other_entering = swap(entering, "pair", 1)
        (own,) = call(
            inverse_kernel,
            (side_of, last),
            (new, swap(sent, "tm", 1), own, *tables),
            [own.shape],
            [own.shape],
        )
        if more:
            side = own_side(own)
            other_entering, side = lax.optimization_barrier((other_entering, side))
            other_kept, other_sent = both_steps(other_odd, other_entering, *other_sides)
            other_came = swap(other_sent, "tm", 1)
    return own[None, None]


def solution(mesh):
    in_specs = (P("pair", "tm", None, None), P("pair", "tm", None, None), P(), P(), P(), P(), P())
    out_specs = P("pair", "tm", None, None)
    return jax.shard_map(
        on_device, mesh=mesh, in_specs=in_specs, out_specs=out_specs, check_vma=False
    )
```

```python
import functools
import math

import jax
import jax.numpy as jnp
import ml_dtypes
import numpy as np
from jax import lax
from jax.experimental import pallas as pl
from jax.experimental.pallas import tpu as pltpu
from jax.sharding import PartitionSpec as P

ITERS = 2

gamma_inv = 0.5


def cas_table(length):
    places = np.arange(length)
    angles = (places[:, None] * places[None, :] % length) * (2.0 * np.pi / length)
    table = np.cos(angles) + np.sin(angles)
    high = table.astype(ml_dtypes.bfloat16)
    low = (table - high.astype(np.float64)).astype(ml_dtypes.bfloat16)
    return jnp.asarray(np.stack([high, low]))


def eigenvalues(length):
    return jnp.asarray((4.0 * np.sin(np.arange(length) * (np.pi / length)) ** 2).astype(np.float32))


def split(values):
    high = values.astype(jnp.bfloat16)
    return high, (values - high.astype(jnp.float32)).astype(jnp.bfloat16)


def parts(table_ref):
    return table_ref[0], table_ref[1]


def product(left, right):
    def one(a, b):
        return jnp.dot(a, b, preferred_element_type=jnp.float32)

    return one(left[0], right[0]) + (one(left[0], right[1]) + one(left[1], right[0]))


def roll(values, shift, axis):
    return pltpu.roll(values, shift % values.shape[axis], axis)


def own_kernel(mean_ref, shift_ref, adjoint_ref, last_ref, own_ref, source_ref, diffusion_ref, reaction_ref, out_ref):
    last = last_ref[0] == 1
    mean = jnp.where(last, 0.0, mean_ref[0])
    shift = jnp.where(last, -1.0, shift_ref[0])
    cells, own = diffusion_ref[...], own_ref[...]
    east = 0.5 * (cells + roll(cells, -1, 0)) - mean
    north = 0.5 * (cells + roll(cells, -1, 1)) - mean
    flux_x = east * (roll(own, -1, 0) - own)
    flux_y = north * (roll(own, -1, 1) - own)
    spread = flux_x - roll(flux_x, 1, 0) + flux_y - roll(flux_y, 1, 1)
    cube = jnp.where(adjoint_ref[0] == 1, 0.0, 1.0) * (reaction_ref[...] * own * own * own)
    out_ref[...] = source_ref[...] + (spread + shift * own - cube)


def gather_halves(core, work_ref, kept_ref, came_ref):
    half = kept_ref.shape[0]
    work_ref[pl.ds(pl.multiple_of(core * half, half), half), :] = kept_ref[...]
    work_ref[pl.ds(pl.multiple_of((1 - core) * half, half), half), :] = came_ref[...]
    return split(work_ref[...])


def row_halves(count):
    return slice(0, count // 2), slice(count // 2, count)


def both_sides(x_ref, middle, y_table, place):
    return product(split(product((x_ref[0, place], x_ref[1, place]), middle)), y_table)


def half_rows(core, half):
    return pl.ds(pl.multiple_of(core * half, half), half)


def send_half(scale, adjoint, core, side, own, partner, reaction, x_ref, y_ref, side_ref, send_ref):
    adjoint_part = 3.0 * reaction * partner * partner * own - partner
    side = side - jnp.where(adjoint, adjoint_part, gamma_inv * partner)
    place = half_rows(1 - core, send_ref.shape[0])
    send_ref[...] = both_sides(x_ref, split(side), parts(y_ref), place) * scale
    side_ref[...] = side


def keep_kernel(scale, core_ref, side_ref, x_ref, y_ref, keep_ref):
    place = half_rows(core_ref[0], keep_ref.shape[0])
    keep_ref[...] = both_sides(x_ref, split(side_ref[...]), parts(y_ref), place) * scale


def first_kernel(
    scale, adjoint_ref, core_ref, own_side_ref, own_ref, partner_ref, reaction_ref, x_ref, y_ref, side_ref, send_ref
):
    send_half(
        scale, adjoint_ref[0] == 1, core_ref[0], own_side_ref[...], own_ref[...], partner_ref[...], reaction_ref[...],
        x_ref, y_ref, side_ref, send_ref,
    )


def later_kernel(
    scale, adjoint_ref, core_ref, partner_last_ref,
    own_side_ref, own_ref, kept_ref, came_ref, former_ref, reaction_ref, x_ref, y_ref,
    side_ref, send_ref, *refs,
):
    modes = gather_halves(core_ref[0], refs[-1], kept_ref, came_ref)
    former = jnp.where(partner_last_ref[0] == 1, 1.0, 0.0) * former_ref[...]
    partner = former + both_sides(x_ref, modes, parts(y_ref), slice(None))
    if len(refs) > 1:
        refs[0][...] = partner
    send_half(
        scale, adjoint_ref[0] == 1, core_ref[0], own_side_ref[...], own_ref[...], partner, reaction_ref[...],
        x_ref, y_ref, side_ref, send_ref,
    )


def inverse_kernel(core_ref, last_ref, kept_ref, came_ref, own_ref, x_ref, y_ref, out_ref, work_ref):
    modes = gather_halves(core_ref[0], work_ref, kept_ref, came_ref)
    former = jnp.where(last_ref[0] == 1, 1.0, 0.0)
    for place in row_halves(work_ref.shape[0]):
        out_ref[place, :] = former * own_ref[place, :] + both_sides(x_ref, modes, parts(y_ref), place)


def steps_kernel(odd_ref, entering_ref, kept_ref, came_ref, rate_ref, new_ref, sent_ref):
    odd = odd_ref[0] == 1
    kept, came, rate = kept_ref[...], came_ref[...], rate_ref[...]
    first = rate * (entering_ref[...] + jnp.where(odd, came, kept))
    second = rate * (first + jnp.where(odd, kept, came))
    new_ref[...] = jnp.where(odd, second, first)
    sent_ref[...] = jnp.where(odd, first, second)


def call(kernel, scalars, arrays, out_shapes, scratch=(), flops=0):
    spec_scalar = pl.BlockSpec(memory_space=pltpu.SMEM)
    spec_array = pl.BlockSpec(memory_space=pltpu.VMEM)
    return pl.pallas_call(
        kernel,
        out_shape=[jax.ShapeDtypeStruct(shape, jnp.float32) for shape in out_shapes],
        in_specs=[spec_scalar] * len(scalars) + [spec_array] * len(arrays),
        out_specs=[spec_array] * len(out_shapes),
        scratch_shapes=[pltpu.VMEM(shape, jnp.float32) for shape in scratch],
        compiler_params=pltpu.CompilerParams(vmem_limit_bytes=16 * 1024 * 1024),
    )(*scalars, *arrays)


def swap(values, axis, mask):
    return lax.ppermute(values, axis, [(i, i ^ mask) for i in range(lax.axis_size(axis))])


def power(base, exponent):
    result = None
    while exponent:
        if exponent & 1:
            result = base if result is None else result * base
        base, exponent = base * base, exponent >> 1
    return result


def pick(options, index):
    result = options[0]
    for number in range(1, len(options)):
        result = jnp.where(index == number, options[number], result)
    return result


def scan_factors(rate, alpha, place, total):
    none = jnp.zeros_like(rate)
    pair = (pick([rate * rate, rate], place & 1), pick([rate, rate * rate], place & 1))
    all_masks, levels, reach = [], [], None
    bit, steps = 1, 2
    while steps < total:
        count = 4 if steps * 4 <= total else 2
        numbers = [2, 3, 1] if count == 4 else [1]
        masks = [number << bit for number in numbers]
        if count == 2 and bit > 1:
            masks = [(1 << bit) | (1 << (bit - 1))]
        factor = power(rate, steps)
        powers = [jnp.ones_like(rate)]
        for _ in range(count - 1):
            powers.append(powers[-1] * factor)
        mine = (place >> bit) & (count - 1)
        join = [pick(powers[::-1], mine ^ number) for number in [0] + numbers]
        enter = [pick([none] + powers, jnp.maximum(mine - (mine ^ number), 0)) for number in [0] + numbers]
        through = pick(powers, mine)
        bit, steps = bit + count.bit_length() - 1, steps * count
        if steps == total:
            round_trip = alpha / (1.0 - alpha * power(rate, total)) * through
            enter = [round_trip * one + two for one, two in zip(join, enter)]
        if reach is not None:
            enter = [reach * one for one in enter]
        reach = through if reach is None else reach * through
        all_masks.append(masks)
        levels.append((join, enter))
    pair, levels = lax.optimization_barrier((pair, levels))
    return pair, [(masks, *level) for masks, level in zip(all_masks, levels)]


def carry_in(kept, came, pair, levels, share):
    others = [swap(kept, "pair", 1), swap(came, "pair", 1)] if share else [None, None]
    carry = pair[0] * kept + pair[1] * came
    entering = jnp.zeros_like(carry)
    for masks, join, enter in levels[:-1]:
        pieces = [carry] + [swap(carry, "tm", mask) for mask in masks]
        carry = sum(one * piece for one, piece in zip(join, pieces))
        entering = entering + sum(one * piece for one, piece in zip(enter, pieces))
    carry, others[0] = lax.optimization_barrier((carry, others[0]))
    masks, _, enter = levels[-1]
    entering = lax.optimization_barrier(entering + enter[0] * carry)
    entering = entering + sum(one * swap(carry, "tm", mask) for one, mask in zip(enter[1:], masks))
    return lax.optimization_barrier((entering, others))


def on_device(fields, forcing, diffusion, reaction, wrap_factor, mean_diffusion, spectral_shift):
    total = lax.axis_size("tm")
    own, source = fields[0, 0], forcing[0, 0]
    grid_x, grid_y = own.shape
    half = grid_x // 2
    scale = 1.0 / (grid_x * grid_y)
    tables = cas_table(grid_x), cas_table(grid_y)
    group, step = lax.axis_index("pair"), lax.axis_index("tm")
    place = jnp.where(group == 1, total - 1 - step, step)
    other_place = total - 1 - place
    core = step & 1

    def scalar(value):
        return value.astype(jnp.int32).reshape(1)

    adjoint, side_of = scalar(group), scalar(core)
    odd, other_odd = scalar(place & 1), scalar(other_place & 1)
    last, other_last = scalar(place == total - 1), scalar(other_place == total - 1)
    eigen_x = lax.dynamic_slice_in_dim(eigenvalues(grid_x), core * half, half, 0)
    rate = 1.0 / (1.0 + spectral_shift + mean_diffusion * (eigen_x[:, None] + eigenvalues(grid_y)[None, :]))
    pair, levels = scan_factors(rate, wrap_factor, place, total)

    def own_side(own):
        (side,) = call(
            own_kernel,
            (mean_diffusion, spectral_shift, adjoint, last),
            (own, source, diffusion, reaction),
            [own.shape],
        )
        return side

    def both_steps(odd, entering, kept, came):
        return call(steps_kernel, (odd,), (entering, kept, came, rate), [kept.shape] * 2)

    partner = [swap(own, "pair", 1)]
    side = own_side(own)
    for iteration in range(ITERS):
        more = iteration + 1 < ITERS
        if iteration == 0:
            side, sent = call(
                functools.partial(first_kernel, scale),
                (adjoint, side_of),
                (side, own, *partner, reaction, *tables),
                [own.shape, (half, grid_y)],
            )
        else:
            side, sent, *partner = call(
                functools.partial(later_kernel, scale),
                (adjoint, side_of, other_last),
                (side, own, other_kept, other_came, *partner, reaction, *tables),
                [own.shape, (half, grid_y)] + [own.shape] * more,
                [own.shape],
            )
        came = swap(sent, "tm", 1)
        (kept,) = call(functools.partial(keep_kernel, scale), (side_of,), (side, *tables), [(half, grid_y)])
        entering, other_sides = carry_in(kept, came, pair, levels, more)
        new, sent = both_steps(odd, entering, kept, came)
        if more:
            other_entering = swap(entering, "pair", 1)
        (own,) = call(
            inverse_kernel,
            (side_of, last),
            (new, swap(sent, "tm", 1), own, *tables),
            [own.shape],
            [own.shape],
        )
        if more:
            side = own_side(own)
            other_entering, side = lax.optimization_barrier((other_entering, side))
            other_kept, other_sent = both_steps(other_odd, other_entering, *other_sides)
            other_came = swap(other_sent, "tm", 1)
    return own[None, None]


def solution(mesh):
    in_specs = (P("pair", "tm", None, None), P("pair", "tm", None, None), P(), P(), P(), P(), P())
    out_specs = P("pair", "tm", None, None)
    return jax.shard_map(
        on_device, mesh=mesh, in_specs=in_specs, out_specs=out_specs, check_vma=False
    )
```

```python
import functools
import math

import jax
import jax.numpy as jnp
import ml_dtypes
import numpy as np
from jax import lax
from jax.experimental import pallas as pl
from jax.experimental.pallas import tpu as pltpu
from jax.sharding import PartitionSpec as P

ITERS = 2

gamma_inv = 0.5


def cas_table(length):
    places = np.arange(length)
    angles = (places[:, None] * places[None, :] % length) * (2.0 * np.pi / length)
    table = np.cos(angles) + np.sin(angles)
    high = table.astype(ml_dtypes.bfloat16)
    low = (table - high.astype(np.float64)).astype(ml_dtypes.bfloat16)
    return jnp.asarray(np.stack([high, low]))


def eigenvalues(length):
    return jnp.asarray((4.0 * np.sin(np.arange(length) * (np.pi / length)) ** 2).astype(np.float32))


def split(values):
    high = values.astype(jnp.bfloat16)
    return high, (values - high.astype(jnp.float32)).astype(jnp.bfloat16)


def parts(table_ref):
    return table_ref[0], table_ref[1]


def product(left, right):
    def one(a, b):
        return jnp.dot(a, b, preferred_element_type=jnp.float32)

    return one(left[0], right[0]) + (one(left[0], right[1]) + one(left[1], right[0]))


def roll(values, shift, axis):
    return pltpu.roll(values, shift % values.shape[axis], axis)


def own_kernel(mean_ref, shift_ref, adjoint_ref, last_ref, own_ref, source_ref, diffusion_ref, reaction_ref, out_ref):
    last = last_ref[0] == 1
    mean = jnp.where(last, 0.0, mean_ref[0])
    shift = jnp.where(last, -1.0, shift_ref[0])
    cells, own = diffusion_ref[...], own_ref[...]
    east = 0.5 * (cells + roll(cells, -1, 0)) - mean
    north = 0.5 * (cells + roll(cells, -1, 1)) - mean
    flux_x = east * (roll(own, -1, 0) - own)
    flux_y = north * (roll(own, -1, 1) - own)
    spread = flux_x - roll(flux_x, 1, 0) + flux_y - roll(flux_y, 1, 1)
    cube = jnp.where(adjoint_ref[0] == 1, 0.0, 1.0) * (reaction_ref[...] * own * own * own)
    out_ref[...] = source_ref[...] + (spread + shift * own - cube)


def gather_halves(core, work_ref, kept_ref, came_ref):
    half = kept_ref.shape[0]
    work_ref[pl.ds(pl.multiple_of(core * half, half), half), :] = kept_ref[...]
    work_ref[pl.ds(pl.multiple_of((1 - core) * half, half), half), :] = came_ref[...]
    return split(work_ref[...])


def row_halves(count):
    return slice(0, count // 2), slice(count // 2, count)


def both_sides(x_ref, middle, y_table, place):
    return product(split(product((x_ref[0, place], x_ref[1, place]), middle)), y_table)


def half_rows(core, half):
    return pl.ds(pl.multiple_of(core * half, half), half)


def send_half(scale, adjoint, core, side, own, partner, reaction, x_ref, y_ref, side_ref, send_ref):
    adjoint_part = 3.0 * reaction * partner * partner * own - partner
    side = side - jnp.where(adjoint, adjoint_part, gamma_inv * partner)
    place = half_rows(1 - core, send_ref.shape[0])
    send_ref[...] = both_sides(x_ref, split(side), parts(y_ref), place) * scale
    side_ref[...] = side


def keep_kernel(scale, core_ref, side_ref, x_ref, y_ref, keep_ref):
    place = half_rows(core_ref[0], keep_ref.shape[0])
    keep_ref[...] = both_sides(x_ref, split(side_ref[...]), parts(y_ref), place) * scale


def first_kernel(
    scale, adjoint_ref, core_ref, own_side_ref, own_ref, partner_ref, reaction_ref, x_ref, y_ref, side_ref, send_ref
):
    send_half(
        scale, adjoint_ref[0] == 1, core_ref[0], own_side_ref[...], own_ref[...], partner_ref[...], reaction_ref[...],
        x_ref, y_ref, side_ref, send_ref,
    )


def later_kernel(
    scale, adjoint_ref, core_ref, partner_last_ref,
    own_side_ref, own_ref, kept_ref, came_ref, former_ref, reaction_ref, x_ref, y_ref,
    side_ref, send_ref, *refs,
):
    modes = gather_halves(core_ref[0], refs[-1], kept_ref, came_ref)
    former = jnp.where(partner_last_ref[0] == 1, 1.0, 0.0) * former_ref[...]
    partner = former + both_sides(x_ref, modes, parts(y_ref), slice(None))
    if len(refs) > 1:
        refs[0][...] = partner
    send_half(
        scale, adjoint_ref[0] == 1, core_ref[0], own_side_ref[...], own_ref[...], partner, reaction_ref[...],
        x_ref, y_ref, side_ref, send_ref,
    )


def inverse_kernel(core_ref, last_ref, kept_ref, came_ref, own_ref, x_ref, y_ref, out_ref, work_ref):
    modes = gather_halves(core_ref[0], work_ref, kept_ref, came_ref)
    former = jnp.where(last_ref[0] == 1, 1.0, 0.0)
    for place in row_halves(work_ref.shape[0]):
        out_ref[place, :] = former * own_ref[place, :] + both_sides(x_ref, modes, parts(y_ref), place)


def steps_kernel(odd_ref, entering_ref, kept_ref, came_ref, rate_ref, new_ref, sent_ref):
    odd = odd_ref[0] == 1
    kept, came, rate = kept_ref[...], came_ref[...], rate_ref[...]
    first = rate * (entering_ref[...] + jnp.where(odd, came, kept))
    second = rate * (first + jnp.where(odd, kept, came))
    new_ref[...] = jnp.where(odd, second, first)
    sent_ref[...] = jnp.where(odd, first, second)


def call(kernel, scalars, arrays, out_shapes, scratch=(), flops=0):
    spec_scalar = pl.BlockSpec(memory_space=pltpu.SMEM)
    spec_array = pl.BlockSpec(memory_space=pltpu.VMEM)
    return pl.pallas_call(
        kernel,
        out_shape=[jax.ShapeDtypeStruct(shape, jnp.float32) for shape in out_shapes],
        in_specs=[spec_scalar] * len(scalars) + [spec_array] * len(arrays),
        out_specs=[spec_array] * len(out_shapes),
        scratch_shapes=[pltpu.VMEM(shape, jnp.float32) for shape in scratch],
        compiler_params=pltpu.CompilerParams(vmem_limit_bytes=16 * 1024 * 1024),
    )(*scalars, *arrays)


def swap(values, axis, mask):
    masks = mask if isinstance(mask, tuple) else (mask, mask)
    return lax.ppermute(values, axis, [(i, i ^ masks[i & 1]) for i in range(lax.axis_size(axis))])


def power(base, exponent):
    result = None
    while exponent:
        if exponent & 1:
            result = base if result is None else result * base
        base, exponent = base * base, exponent >> 1
    return result


def pick(options, index):
    result = options[0]
    for number in range(1, len(options)):
        result = jnp.where(index == number, options[number], result)
    return result


def scan_factors(rate, alpha, place, core, total):
    none = jnp.zeros_like(rate)
    pair = (pick([rate * rate, rate], place & 1), pick([rate, rate * rate], place & 1))
    all_masks, levels, reach = [], [], None
    bit, steps = 1, 2
    while steps < total:
        count = 4 if steps * 4 <= total else 2
        numbers = [(3, 3), (2, 1), (1, 2)] if count == 4 else [(1, 1)]
        masks = [(even << bit, odd << bit) for even, odd in numbers]
        if count == 2 and bit > 1:
            masks = [((1 << bit) | (1 << (bit - 1)),) * 2]
        factor = power(rate, steps)
        powers = [jnp.ones_like(rate)]
        for _ in range(count - 1):
            powers.append(powers[-1] * factor)
        mine = (place >> bit) & (count - 1)
        others = [mine ^ jnp.where(core == 1, odd, even) for even, odd in [(0, 0)] + numbers]
        join = [pick(powers[::-1], other) for other in others]
        enter = [pick([none] + powers, jnp.maximum(mine - other, 0)) for other in others]
        through = pick(powers, mine)
        bit, steps = bit + count.bit_length() - 1, steps * count
        if steps == total:
            round_trip = alpha / (1.0 - alpha * power(rate, total)) * through
            enter = [round_trip * one + two for one, two in zip(join, enter)]
        if reach is not None:
            enter = [reach * one for one in enter]
        reach = through if reach is None else reach * through
        all_masks.append(masks)
        levels.append((join, enter))
    pair, levels = lax.optimization_barrier((pair, levels))
    return pair, [(masks, *level) for masks, level in zip(all_masks, levels)]


def carry_in(kept, came, pair, levels, share):
    others = [swap(kept, "pair", 1), swap(came, "pair", 1)] if share else [None, None]
    carry = pair[0] * kept + pair[1] * came
    entering = jnp.zeros_like(carry)
    for masks, join, enter in levels[:-1]:
        pieces = [carry] + [swap(carry, "tm", mask) for mask in masks]
        carry = sum(one * piece for one, piece in zip(join, pieces))
        entering = entering + sum(one * piece for one, piece in zip(enter, pieces))
    carry, others[0] = lax.optimization_barrier((carry, others[0]))
    masks, _, enter = levels[-1]
    entering = lax.optimization_barrier(entering + enter[0] * carry)
    entering = entering + sum(one * swap(carry, "tm", mask) for one, mask in zip(enter[1:], masks))
    return lax.optimization_barrier((entering, others))


def on_device(fields, forcing, diffusion, reaction, wrap_factor, mean_diffusion, spectral_shift):
    total = lax.axis_size("tm")
    own, source = fields[0, 0], forcing[0, 0]
    grid_x, grid_y = own.shape
    half = grid_x // 2
    scale = 1.0 / (grid_x * grid_y)
    tables = cas_table(grid_x), cas_table(grid_y)
    group, step = lax.axis_index("pair"), lax.axis_index("tm")
    place = jnp.where(group == 1, total - 1 - step, step)
    other_place = total - 1 - place
    core = step & 1

    def scalar(value):
        return value.astype(jnp.int32).reshape(1)

    adjoint, side_of = scalar(group), scalar(core)
    odd, other_odd = scalar(place & 1), scalar(other_place & 1)
    last, other_last = scalar(place == total - 1), scalar(other_place == total - 1)
    eigen_x = lax.dynamic_slice_in_dim(eigenvalues(grid_x), core * half, half, 0)
    rate = 1.0 / (1.0 + spectral_shift + mean_diffusion * (eigen_x[:, None] + eigenvalues(grid_y)[None, :]))
    pair, levels = scan_factors(rate, wrap_factor, place, core, total)

    def own_side(own):
        (side,) = call(
            own_kernel,
            (mean_diffusion, spectral_shift, adjoint, last),
            (own, source, diffusion, reaction),
            [own.shape],
        )
        return side

    def both_steps(odd, entering, kept, came):
        return call(steps_kernel, (odd,), (entering, kept, came, rate), [kept.shape] * 2)

    partner = [swap(own, "pair", 1)]
    side = own_side(own)
    for iteration in range(ITERS):
        more = iteration + 1 < ITERS
        if iteration == 0:
            side, sent = call(
                functools.partial(first_kernel, scale),
                (adjoint, side_of),
                (side, own, *partner, reaction, *tables),
                [own.shape, (half, grid_y)],
            )
        else:
            side, sent, *partner = call(
                functools.partial(later_kernel, scale),
                (adjoint, side_of, other_last),
                (side, own, other_kept, other_came, *partner, reaction, *tables),
                [own.shape, (half, grid_y)] + [own.shape] * more,
                [own.shape],
            )
        came = swap(sent, "tm", 1)
        (kept,) = call(functools.partial(keep_kernel, scale), (side_of,), (side, *tables), [(half, grid_y)])
        entering, other_sides = carry_in(kept, came, pair, levels, more)
        new, sent = both_steps(odd, entering, kept, came)
        if more:
            other_entering = swap(entering, "pair", 1)
        (own,) = call(
            inverse_kernel,
            (side_of, last),
            (new, swap(sent, "tm", 1), own, *tables),
            [own.shape],
            [own.shape],
        )
        if more:
            side = own_side(own)
            other_entering, side = lax.optimization_barrier((other_entering, side))
            other_kept, other_sent = both_steps(other_odd, other_entering, *other_sides)
            other_came = swap(other_sent, "tm", 1)
    return own[None, None]


def solution(mesh):
    in_specs = (P("pair", "tm", None, None), P("pair", "tm", None, None), P(), P(), P(), P(), P())
    out_specs = P("pair", "tm", None, None)
    return jax.shard_map(
        on_device, mesh=mesh, in_specs=in_specs, out_specs=out_specs, check_vma=False
    )
```

```python
import functools
import math

import jax
import jax.numpy as jnp
import ml_dtypes
import numpy as np
from jax import lax
from jax.experimental import pallas as pl
from jax.experimental.pallas import tpu as pltpu
from jax.sharding import PartitionSpec as P

ITERS = 2

gamma_inv = 0.5


def cas_table(length):
    places = np.arange(length)
    angles = (places[:, None] * places[None, :] % length) * (2.0 * np.pi / length)
    table = np.cos(angles) + np.sin(angles)
    high = table.astype(ml_dtypes.bfloat16)
    low = (table - high.astype(np.float64)).astype(ml_dtypes.bfloat16)
    return jnp.asarray(np.stack([high, low]))


def eigenvalues(length):
    return jnp.asarray((4.0 * np.sin(np.arange(length) * (np.pi / length)) ** 2).astype(np.float32))


def split(values):
    high = values.astype(jnp.bfloat16)
    return high, (values - high.astype(jnp.float32)).astype(jnp.bfloat16)


def parts(table_ref):
    return table_ref[0], table_ref[1]


def product(left, right):
    def one(a, b):
        return jnp.dot(a, b, preferred_element_type=jnp.float32)

    return one(left[0], right[0]) + (one(left[0], right[1]) + one(left[1], right[0]))


def roll(values, shift, axis):
    return pltpu.roll(values, shift % values.shape[axis], axis)


def own_kernel(mean_ref, shift_ref, adjoint_ref, last_ref, own_ref, source_ref, diffusion_ref, reaction_ref, out_ref):
    last = last_ref[0] == 1
    mean = jnp.where(last, 0.0, mean_ref[0])
    shift = jnp.where(last, -1.0, shift_ref[0])
    cells, own = diffusion_ref[...], own_ref[...]
    east = 0.5 * (cells + roll(cells, -1, 0)) - mean
    north = 0.5 * (cells + roll(cells, -1, 1)) - mean
    flux_x = east * (roll(own, -1, 0) - own)
    flux_y = north * (roll(own, -1, 1) - own)
    spread = flux_x - roll(flux_x, 1, 0) + flux_y - roll(flux_y, 1, 1)
    cube = jnp.where(adjoint_ref[0] == 1, 0.0, 1.0) * (reaction_ref[...] * own * own * own)
    out_ref[...] = source_ref[...] + (spread + shift * own - cube)


def gather_halves(core, work_ref, kept_ref, came_ref):
    half = kept_ref.shape[0]
    work_ref[pl.ds(pl.multiple_of(core * half, half), half), :] = kept_ref[...]
    work_ref[pl.ds(pl.multiple_of((1 - core) * half, half), half), :] = came_ref[...]
    return split(work_ref[...])


def row_halves(count):
    return slice(0, count // 2), slice(count // 2, count)


def both_sides(x_ref, middle, y_table, place):
    return product(split(product((x_ref[0, place], x_ref[1, place]), middle)), y_table)


def half_rows(core, half):
    return pl.ds(pl.multiple_of(core * half, half), half)


def send_half(scale, adjoint, core, side, own, partner, reaction, x_ref, y_ref, side_ref, send_ref):
    adjoint_part = 3.0 * reaction * partner * partner * own - partner
    side = side - jnp.where(adjoint, adjoint_part, gamma_inv * partner)
    place = half_rows(1 - core, send_ref.shape[0])
    send_ref[...] = both_sides(x_ref, split(side), parts(y_ref), place) * scale
    side_ref[...] = side


def keep_kernel(scale, core_ref, side_ref, x_ref, y_ref, keep_ref):
    place = half_rows(core_ref[0], keep_ref.shape[0])
    keep_ref[...] = both_sides(x_ref, split(side_ref[...]), parts(y_ref), place) * scale


def first_kernel(
    scale, adjoint_ref, core_ref, own_side_ref, own_ref, partner_ref, reaction_ref, x_ref, y_ref, side_ref, send_ref
):
    send_half(
        scale, adjoint_ref[0] == 1, core_ref[0], own_side_ref[...], own_ref[...], partner_ref[...], reaction_ref[...],
        x_ref, y_ref, side_ref, send_ref,
    )


def later_kernel(
    scale, adjoint_ref, core_ref, partner_last_ref,
    own_side_ref, own_ref, kept_ref, came_ref, former_ref, reaction_ref, x_ref, y_ref,
    side_ref, send_ref, *refs,
):
    modes = gather_halves(core_ref[0], refs[-1], kept_ref, came_ref)
    former = jnp.where(partner_last_ref[0] == 1, 1.0, 0.0) * former_ref[...]
    partner = former + both_sides(x_ref, modes, parts(y_ref), slice(None))
    if len(refs) > 1:
        refs[0][...] = partner
    send_half(
        scale, adjoint_ref[0] == 1, core_ref[0], own_side_ref[...], own_ref[...], partner, reaction_ref[...],
        x_ref, y_ref, side_ref, send_ref,
    )


def inverse_kernel(core_ref, last_ref, kept_ref, came_ref, own_ref, x_ref, y_ref, out_ref, work_ref):
    modes = gather_halves(core_ref[0], work_ref, kept_ref, came_ref)
    former = jnp.where(last_ref[0] == 1, 1.0, 0.0)
    for place in row_halves(work_ref.shape[0]):
        out_ref[place, :] = former * own_ref[place, :] + both_sides(x_ref, modes, parts(y_ref), place)


def steps_kernel(odd_ref, entering_ref, kept_ref, came_ref, rate_ref, new_ref, sent_ref):
    odd = odd_ref[0] == 1
    kept, came, rate = kept_ref[...], came_ref[...], rate_ref[...]
    first = rate * (entering_ref[...] + jnp.where(odd, came, kept))
    second = rate * (first + jnp.where(odd, kept, came))
    new_ref[...] = jnp.where(odd, second, first)
    sent_ref[...] = jnp.where(odd, first, second)


def call(kernel, scalars, arrays, out_shapes, scratch=(), flops=0):
    spec_scalar = pl.BlockSpec(memory_space=pltpu.SMEM)
    spec_array = pl.BlockSpec(memory_space=pltpu.VMEM)
    return pl.pallas_call(
        kernel,
        out_shape=[jax.ShapeDtypeStruct(shape, jnp.float32) for shape in out_shapes],
        in_specs=[spec_scalar] * len(scalars) + [spec_array] * len(arrays),
        out_specs=[spec_array] * len(out_shapes),
        scratch_shapes=[pltpu.VMEM(shape, jnp.float32) for shape in scratch],
        compiler_params=pltpu.CompilerParams(vmem_limit_bytes=16 * 1024 * 1024),
    )(*scalars, *arrays)


def swap(values, axis, mask):
    masks = mask if isinstance(mask, tuple) else (mask, mask)
    return lax.ppermute(values, axis, [(i, i ^ masks[i & 1]) for i in range(lax.axis_size(axis))])


def power(base, exponent):
    result = None
    while exponent:
        if exponent & 1:
            result = base if result is None else result * base
        base, exponent = base * base, exponent >> 1
    return result


def pick(options, index):
    result = options[0]
    for number in range(1, len(options)):
        result = jnp.where(index == number, options[number], result)
    return result


def scan_factors(rate, alpha, place, core, total):
    none = jnp.zeros_like(rate)
    pair = (pick([rate * rate, rate], place & 1), pick([rate, rate * rate], place & 1))
    all_masks, levels, reach = [], [], None
    bit, steps = 1, 2
    while steps < total:
        count = 4 if steps * 4 <= total else 2
        numbers = [(3, 3), (2, 1), (1, 2)] if count == 4 else [(1, 1)]
        masks = [(even << bit, odd << bit) for even, odd in numbers]
        if count == 2 and bit > 1:
            masks = [((1 << bit) | (1 << (bit - 1)),) * 2]
        factor = power(rate, steps)
        powers = [jnp.ones_like(rate)]
        for _ in range(count - 1):
            powers.append(powers[-1] * factor)
        mine = (place >> bit) & (count - 1)
        others = [mine ^ jnp.where(core == 1, odd, even) for even, odd in [(0, 0)] + numbers]
        join = [pick(powers[::-1], other) for other in others]
        enter = [pick([none] + powers, jnp.maximum(mine - other, 0)) for other in others]
        through = pick(powers, mine)
        bit, steps = bit + count.bit_length() - 1, steps * count
        if steps == total:
            round_trip = alpha / (1.0 - alpha * power(rate, total)) * through
            enter = [round_trip * one + two for one, two in zip(join, enter)]
        if reach is not None:
            enter = [reach * one for one in enter]
        reach = through if reach is None else reach * through
        all_masks.append(masks)
        levels.append((join, enter))
    pair, levels = lax.optimization_barrier((pair, levels))
    return pair, [(masks, *level) for masks, level in zip(all_masks, levels)]


def carry_in(kept, came, pair, levels, share):
    others = [swap(kept, "pair", 1), swap(came, "pair", 1)] if share else [None, None]
    carry = pair[0] * kept + pair[1] * came
    entering = jnp.zeros_like(carry)
    for masks, join, enter in levels[:-1]:
        pieces = [carry] + [swap(carry, "tm", mask) for mask in masks]
        carry = sum(one * piece for one, piece in zip(join, pieces))
        entering = entering + sum(one * piece for one, piece in zip(enter, pieces))
    carry = lax.optimization_barrier(carry)
    masks, _, enter = levels[-1]
    entering, others = lax.optimization_barrier((entering + enter[0] * carry, others))
    entering = entering + sum(one * swap(carry, "tm", mask) for one, mask in zip(enter[1:], masks))
    return lax.optimization_barrier((entering, others))


def on_device(fields, forcing, diffusion, reaction, wrap_factor, mean_diffusion, spectral_shift):
    total = lax.axis_size("tm")
    own, source = fields[0, 0], forcing[0, 0]
    grid_x, grid_y = own.shape
    half = grid_x // 2
    scale = 1.0 / (grid_x * grid_y)
    tables = cas_table(grid_x), cas_table(grid_y)
    group, step = lax.axis_index("pair"), lax.axis_index("tm")
    place = jnp.where(group == 1, total - 1 - step, step)
    other_place = total - 1 - place
    core = step & 1

    def scalar(value):
        return value.astype(jnp.int32).reshape(1)

    adjoint, side_of = scalar(group), scalar(core)
    odd, other_odd = scalar(place & 1), scalar(other_place & 1)
    last, other_last = scalar(place == total - 1), scalar(other_place == total - 1)
    eigen_x = lax.dynamic_slice_in_dim(eigenvalues(grid_x), core * half, half, 0)
    rate = 1.0 / (1.0 + spectral_shift + mean_diffusion * (eigen_x[:, None] + eigenvalues(grid_y)[None, :]))
    pair, levels = scan_factors(rate, wrap_factor, place, core, total)

    def own_side(own):
        (side,) = call(
            own_kernel,
            (mean_diffusion, spectral_shift, adjoint, last),
            (own, source, diffusion, reaction),
            [own.shape],
        )
        return side

    def both_steps(odd, entering, kept, came):
        return call(steps_kernel, (odd,), (entering, kept, came, rate), [kept.shape] * 2)

    partner = [swap(own, "pair", 1)]
    side = own_side(own)
    for iteration in range(ITERS):
        more = iteration + 1 < ITERS
        if iteration == 0:
            side, sent = call(
                functools.partial(first_kernel, scale),
                (adjoint, side_of),
                (side, own, *partner, reaction, *tables),
                [own.shape, (half, grid_y)],
            )
        else:
            side, sent, *partner = call(
                functools.partial(later_kernel, scale),
                (adjoint, side_of, other_last),
                (side, own, other_kept, other_came, *partner, reaction, *tables),
                [own.shape, (half, grid_y)] + [own.shape] * more,
                [own.shape],
            )
        came = swap(sent, "tm", 1)
        (kept,) = call(functools.partial(keep_kernel, scale), (side_of,), (side, *tables), [(half, grid_y)])
        entering, other_sides = carry_in(kept, came, pair, levels, more)
        new, sent = both_steps(odd, entering, kept, came)
        if more:
            other_entering = swap(entering, "pair", 1)
        (own,) = call(
            inverse_kernel,
            (side_of, last),
            (new, swap(sent, "tm", 1), own, *tables),
            [own.shape],
            [own.shape],
        )
        if more:
            side = own_side(own)
            other_entering, side = lax.optimization_barrier((other_entering, side))
            other_kept, other_sent = both_steps(other_odd, other_entering, *other_sides)
            other_came = swap(other_sent, "tm", 1)
    return own[None, None]


def solution(mesh):
    in_specs = (P("pair", "tm", None, None), P("pair", "tm", None, None), P(), P(), P(), P(), P())
    out_specs = P("pair", "tm", None, None)
    return jax.shard_map(
        on_device, mesh=mesh, in_specs=in_specs, out_specs=out_specs, check_vma=False
    )
```

```python
import functools
import math

import jax
import jax.numpy as jnp
import ml_dtypes
import numpy as np
from jax import lax
from jax.experimental import pallas as pl
from jax.experimental.pallas import tpu as pltpu
from jax.sharding import PartitionSpec as P

ITERS = 2

gamma_inv = 0.5


def cas_table(length):
    places = np.arange(length)
    angles = (places[:, None] * places[None, :] % length) * (2.0 * np.pi / length)
    table = np.cos(angles) + np.sin(angles)
    high = table.astype(ml_dtypes.bfloat16)
    low = (table - high.astype(np.float64)).astype(ml_dtypes.bfloat16)
    return jnp.asarray(np.stack([high, low]))


def eigenvalues(length):
    return jnp.asarray((4.0 * np.sin(np.arange(length) * (np.pi / length)) ** 2).astype(np.float32))


def split(values):
    high = values.astype(jnp.bfloat16)
    return high, (values - high.astype(jnp.float32)).astype(jnp.bfloat16)


def parts(table_ref):
    return table_ref[0], table_ref[1]


def product(left, right):
    def one(a, b):
        return jnp.dot(a, b, preferred_element_type=jnp.float32)

    return one(left[0], right[0]) + (one(left[0], right[1]) + one(left[1], right[0]))


def roll(values, shift, axis):
    return pltpu.roll(values, shift % values.shape[axis], axis)


def own_kernel(mean_ref, shift_ref, adjoint_ref, last_ref, own_ref, source_ref, diffusion_ref, reaction_ref, out_ref):
    last = last_ref[0] == 1
    mean = jnp.where(last, 0.0, mean_ref[0])
    shift = jnp.where(last, -1.0, shift_ref[0])
    cells, own = diffusion_ref[...], own_ref[...]
    east = 0.5 * (cells + roll(cells, -1, 0)) - mean
    north = 0.5 * (cells + roll(cells, -1, 1)) - mean
    flux_x = east * (roll(own, -1, 0) - own)
    flux_y = north * (roll(own, -1, 1) - own)
    spread = flux_x - roll(flux_x, 1, 0) + flux_y - roll(flux_y, 1, 1)
    cube = jnp.where(adjoint_ref[0] == 1, 0.0, 1.0) * (reaction_ref[...] * own * own * own)
    out_ref[...] = source_ref[...] + (spread + shift * own - cube)


def gather_halves(core, work_ref, kept_ref, came_ref):
    half = kept_ref.shape[0]
    work_ref[pl.ds(pl.multiple_of(core * half, half), half), :] = kept_ref[...]
    work_ref[pl.ds(pl.multiple_of((1 - core) * half, half), half), :] = came_ref[...]
    return split(work_ref[...])


def row_halves(count):
    return slice(0, count // 2), slice(count // 2, count)


def both_sides(x_ref, middle, y_table, place):
    return product(split(product((x_ref[0, place], x_ref[1, place]), middle)), y_table)


def half_rows(core, half):
    return pl.ds(pl.multiple_of(core * half, half), half)


def coupled(adjoint, side, own, partner, reaction):
    adjoint_part = 3.0 * reaction * partner * partner * own - partner
    return side - jnp.where(adjoint, adjoint_part, gamma_inv * partner)


def send_half(scale, core, side, x_ref, y_ref, send_ref):
    place = half_rows(1 - core, send_ref.shape[0])
    send_ref[...] = both_sides(x_ref, split(side), parts(y_ref), place) * scale


def keep_kernel(scale, core_ref, side_ref, x_ref, y_ref, keep_ref):
    place = half_rows(core_ref[0], keep_ref.shape[0])
    keep_ref[...] = both_sides(x_ref, split(side_ref[...]), parts(y_ref), place) * scale


def first_kernel(
    scale, adjoint_ref, core_ref, own_side_ref, own_ref, partner_ref, reaction_ref, x_ref, y_ref, side_ref, send_ref
):
    side = coupled(adjoint_ref[0] == 1, own_side_ref[...], own_ref[...], partner_ref[...], reaction_ref[...])
    side_ref[...] = side
    send_half(scale, core_ref[0], side, x_ref, y_ref, send_ref)


def later_kernel(
    scale, adjoint_ref, core_ref, partner_last_ref,
    own_side_ref, own_ref, kept_ref, came_ref, former_ref, reaction_ref, x_ref, y_ref,
    side_ref, send_ref, *refs,
):
    modes = gather_halves(core_ref[0], refs[-1], kept_ref, came_ref)
    former = jnp.where(partner_last_ref[0] == 1, 1.0, 0.0)
    sides = []
    for place in row_halves(own_ref.shape[0]):
        partner = former * former_ref[place, :] + both_sides(x_ref, modes, parts(y_ref), place)
        if len(refs) > 1:
            refs[0][place, :] = partner
        sides.append(
            coupled(adjoint_ref[0] == 1, own_side_ref[place, :], own_ref[place, :], partner, reaction_ref[place, :])
        )
        side_ref[place, :] = sides[-1]
    send_half(scale, core_ref[0], jnp.concatenate(sides, 0), x_ref, y_ref, send_ref)


def inverse_kernel(core_ref, last_ref, kept_ref, came_ref, own_ref, x_ref, y_ref, out_ref, work_ref):
    modes = gather_halves(core_ref[0], work_ref, kept_ref, came_ref)
    former = jnp.where(last_ref[0] == 1, 1.0, 0.0)
    for place in row_halves(work_ref.shape[0]):
        out_ref[place, :] = former * own_ref[place, :] + both_sides(x_ref, modes, parts(y_ref), place)


def steps_kernel(odd_ref, entering_ref, kept_ref, came_ref, rate_ref, new_ref, sent_ref):
    odd = odd_ref[0] == 1
    kept, came, rate = kept_ref[...], came_ref[...], rate_ref[...]
    first = rate * (entering_ref[...] + jnp.where(odd, came, kept))
    second = rate * (first + jnp.where(odd, kept, came))
    new_ref[...] = jnp.where(odd, second, first)
    sent_ref[...] = jnp.where(odd, first, second)


def call(kernel, scalars, arrays, out_shapes, scratch=(), flops=0):
    spec_scalar = pl.BlockSpec(memory_space=pltpu.SMEM)
    spec_array = pl.BlockSpec(memory_space=pltpu.VMEM)
    return pl.pallas_call(
        kernel,
        out_shape=[jax.ShapeDtypeStruct(shape, jnp.float32) for shape in out_shapes],
        in_specs=[spec_scalar] * len(scalars) + [spec_array] * len(arrays),
        out_specs=[spec_array] * len(out_shapes),
        scratch_shapes=[pltpu.VMEM(shape, jnp.float32) for shape in scratch],
        compiler_params=pltpu.CompilerParams(vmem_limit_bytes=16 * 1024 * 1024),
    )(*scalars, *arrays)


def swap(values, axis, mask):
    masks = mask if isinstance(mask, tuple) else (mask, mask)
    return lax.ppermute(values, axis, [(i, i ^ masks[i & 1]) for i in range(lax.axis_size(axis))])


def power(base, exponent):
    result = None
    while exponent:
        if exponent & 1:
            result = base if result is None else result * base
        base, exponent = base * base, exponent >> 1
    return result


def pick(options, index):
    result = options[0]
    for number in range(1, len(options)):
        result = jnp.where(index == number, options[number], result)
    return result


def scan_factors(rate, alpha, place, core, total):
    none = jnp.zeros_like(rate)
    pair = (pick([rate * rate, rate], place & 1), pick([rate, rate * rate], place & 1))
    all_masks, levels, reach = [], [], None
    bit, steps = 1, 2
    while steps < total:
        count = 4 if steps * 4 <= total else 2
        numbers = [(3, 3), (2, 1), (1, 2)] if count == 4 else [(1, 1)]
        masks = [(even << bit, odd << bit) for even, odd in numbers]
        if count == 2 and bit > 1:
            masks = [((1 << bit) | (1 << (bit - 1)),) * 2]
        factor = power(rate, steps)
        powers = [jnp.ones_like(rate)]
        for _ in range(count - 1):
            powers.append(powers[-1] * factor)
        mine = (place >> bit) & (count - 1)
        others = [mine ^ jnp.where(core == 1, odd, even) for even, odd in [(0, 0)] + numbers]
        join = [pick(powers[::-1], other) for other in others]
        enter = [pick([none] + powers, jnp.maximum(mine - other, 0)) for other in others]
        through = pick(powers, mine)
        bit, steps = bit + count.bit_length() - 1, steps * count
        if steps == total:
            round_trip = alpha / (1.0 - alpha * power(rate, total)) * through
            enter = [round_trip * one + two for one, two in zip(join, enter)]
        if reach is not None:
            enter = [reach * one for one in enter]
        reach = through if reach is None else reach * through
        all_masks.append(masks)
        levels.append((join, enter))
    pair, levels = lax.optimization_barrier((pair, levels))
    return pair, [(masks, *level) for masks, level in zip(all_masks, levels)]


def carry_in(kept, came, pair, levels, share):
    others = [swap(kept, "pair", 1), swap(came, "pair", 1)] if share else [None, None]
    carry = pair[0] * kept + pair[1] * came
    entering = jnp.zeros_like(carry)
    for masks, join, enter in levels[:-1]:
        pieces = [carry] + [swap(carry, "tm", mask) for mask in masks]
        carry = sum(one * piece for one, piece in zip(join, pieces))
        entering = entering + sum(one * piece for one, piece in zip(enter, pieces))
    carry = lax.optimization_barrier(carry)
    masks, _, enter = levels[-1]
    entering, others = lax.optimization_barrier((entering + enter[0] * carry, others))
    entering = entering + sum(one * swap(carry, "tm", mask) for one, mask in zip(enter[1:], masks))
    return lax.optimization_barrier((entering, others))


def on_device(fields, forcing, diffusion, reaction, wrap_factor, mean_diffusion, spectral_shift):
    total = lax.axis_size("tm")
    own, source = fields[0, 0], forcing[0, 0]
    grid_x, grid_y = own.shape
    half = grid_x // 2
    scale = 1.0 / (grid_x * grid_y)
    tables = cas_table(grid_x), cas_table(grid_y)
    group, step = lax.axis_index("pair"), lax.axis_index("tm")
    place = jnp.where(group == 1, total - 1 - step, step)
    other_place = total - 1 - place
    core = step & 1

    def scalar(value):
        return value.astype(jnp.int32).reshape(1)

    adjoint, side_of = scalar(group), scalar(core)
    odd, other_odd = scalar(place & 1), scalar(other_place & 1)
    last, other_last = scalar(place == total - 1), scalar(other_place == total - 1)
    eigen_x = lax.dynamic_slice_in_dim(eigenvalues(grid_x), core * half, half, 0)
    rate = 1.0 / (1.0 + spectral_shift + mean_diffusion * (eigen_x[:, None] + eigenvalues(grid_y)[None, :]))
    pair, levels = scan_factors(rate, wrap_factor, place, core, total)

    def own_side(own):
        (side,) = call(
            own_kernel,
            (mean_diffusion, spectral_shift, adjoint, last),
            (own, source, diffusion, reaction),
            [own.shape],
        )
        return side

    def both_steps(odd, entering, kept, came):
        return call(steps_kernel, (odd,), (entering, kept, came, rate), [kept.shape] * 2)

    partner = [swap(own, "pair", 1)]
    side = own_side(own)
    for iteration in range(ITERS):
        more = iteration + 1 < ITERS
        if iteration == 0:
            side, sent = call(
                functools.partial(first_kernel, scale),
                (adjoint, side_of),
                (side, own, *partner, reaction, *tables),
                [own.shape, (half, grid_y)],
            )
        else:
            side, sent, *partner = call(
                functools.partial(later_kernel, scale),
                (adjoint, side_of, other_last),
                (side, own, other_kept, other_came, *partner, reaction, *tables),
                [own.shape, (half, grid_y)] + [own.shape] * more,
                [own.shape],
            )
        came = swap(sent, "tm", 1)
        (kept,) = call(functools.partial(keep_kernel, scale), (side_of,), (side, *tables), [(half, grid_y)])
        entering, other_sides = carry_in(kept, came, pair, levels, more)
        new, sent = both_steps(odd, entering, kept, came)
        if more:
            other_entering = swap(entering, "pair", 1)
        (own,) = call(
            inverse_kernel,
            (side_of, last),
            (new, swap(sent, "tm", 1), own, *tables),
            [own.shape],
            [own.shape],
        )
        if more:
            side = own_side(own)
            other_entering, side = lax.optimization_barrier((other_entering, side))
            other_kept, other_sent = both_steps(other_odd, other_entering, *other_sides)
            other_came = swap(other_sent, "tm", 1)
    return own[None, None]


def solution(mesh):
    in_specs = (P("pair", "tm", None, None), P("pair", "tm", None, None), P(), P(), P(), P(), P())
    out_specs = P("pair", "tm", None, None)
    return jax.shard_map(
        on_device, mesh=mesh, in_specs=in_specs, out_specs=out_specs, check_vma=False
    )
```

```python
import functools
import math

import jax
import jax.numpy as jnp
import ml_dtypes
import numpy as np
from jax import lax
from jax.experimental import pallas as pl
from jax.experimental.pallas import tpu as pltpu
from jax.sharding import PartitionSpec as P

ITERS = 2

gamma_inv = 0.5


def cas_table(length):
    places = np.arange(length)
    angles = (places[:, None] * places[None, :] % length) * (2.0 * np.pi / length)
    table = np.cos(angles) + np.sin(angles)
    high = table.astype(ml_dtypes.bfloat16)
    low = (table - high.astype(np.float64)).astype(ml_dtypes.bfloat16)
    return jnp.asarray(np.stack([high, low]))


def eigenvalues(length):
    return jnp.asarray((4.0 * np.sin(np.arange(length) * (np.pi / length)) ** 2).astype(np.float32))


def split(values):
    high = values.astype(jnp.bfloat16)
    return high, (values - high.astype(jnp.float32)).astype(jnp.bfloat16)


def parts(table_ref):
    return table_ref[0], table_ref[1]


def product(left, right):
    def one(a, b):
        return jnp.dot(a, b, preferred_element_type=jnp.float32)

    return one(left[0], right[0]) + (one(left[0], right[1]) + one(left[1], right[0]))


def roll(values, shift, axis):
    return pltpu.roll(values, shift % values.shape[axis], axis)


def own_kernel(mean_ref, shift_ref, adjoint_ref, last_ref, own_ref, source_ref, diffusion_ref, reaction_ref, out_ref):
    last = last_ref[0] == 1
    mean = jnp.where(last, 0.0, mean_ref[0])
    shift = jnp.where(last, -1.0, shift_ref[0])
    cells, own = diffusion_ref[...], own_ref[...]
    east = 0.5 * (cells + roll(cells, -1, 0)) - mean
    north = 0.5 * (cells + roll(cells, -1, 1)) - mean
    flux_x = east * (roll(own, -1, 0) - own)
    flux_y = north * (roll(own, -1, 1) - own)
    spread = flux_x - roll(flux_x, 1, 0) + flux_y - roll(flux_y, 1, 1)
    cube = jnp.where(adjoint_ref[0] == 1, 0.0, 1.0) * (reaction_ref[...] * own * own * own)
    out_ref[...] = source_ref[...] + (spread + shift * own - cube)


def gather_halves(core, work_ref, kept_ref, came_ref):
    half = kept_ref.shape[0]
    work_ref[pl.ds(pl.multiple_of(core * half, half), half), :] = kept_ref[...]
    work_ref[pl.ds(pl.multiple_of((1 - core) * half, half), half), :] = came_ref[...]
    return split(work_ref[...])


def row_halves(count):
    return slice(0, count // 2), slice(count // 2, count)


def both_sides(x_ref, middle, y_table, place):
    return product(split(product((x_ref[0, place], x_ref[1, place]), middle)), y_table)


def half_rows(core, half):
    return pl.ds(pl.multiple_of(core * half, half), half)


def coupled(adjoint, side, own, partner, reaction):
    adjoint_part = 3.0 * reaction * partner * partner * own - partner
    return side - jnp.where(adjoint, adjoint_part, gamma_inv * partner)


def send_half(scale, core, side, x_ref, y_ref, send_ref):
    place = half_rows(1 - core, send_ref.shape[0])
    send_ref[...] = both_sides(x_ref, split(side), parts(y_ref), place) * scale


def keep_kernel(scale, core_ref, side_ref, x_ref, y_ref, keep_ref):
    place = half_rows(core_ref[0], keep_ref.shape[0])
    keep_ref[...] = both_sides(x_ref, split(side_ref[...]), parts(y_ref), place) * scale


def first_kernel(
    scale, adjoint_ref, core_ref, own_side_ref, own_ref, partner_ref, reaction_ref, x_ref, y_ref, side_ref, send_ref
):
    side = coupled(adjoint_ref[0] == 1, own_side_ref[...], own_ref[...], partner_ref[...], reaction_ref[...])
    side_ref[...] = side
    send_half(scale, core_ref[0], side, x_ref, y_ref, send_ref)


def later_kernel(scale, adjoint_ref, core_ref, last_ref, other_last_ref, reaction_ref, x_ref, y_ref, *refs):
    steps_in, out_refs = (refs[:5], refs[5:10]), refs[10:]
    work_refs = out_refs[-2:]
    place_out = half_rows(core_ref[0], out_refs[0].shape[0])
    for number, (side_ref, own_ref, kept_ref, came_ref, former_ref) in enumerate(steps_in):
        modes = gather_halves(core_ref[0], work_refs[number], kept_ref, came_ref)
        former = jnp.where((last_ref, other_last_ref)[number][0] == 1, 1.0, 0.0)
        sides = []
        for place in row_halves(own_ref.shape[0]):
            partner = former * former_ref[place, :] + both_sides(x_ref, modes, parts(y_ref), place)
            if len(out_refs) > 4:
                out_refs[2 + number][place, :] = partner
            sides.append(
                coupled(adjoint_ref[0] == 1, side_ref[place, :], own_ref[place, :], partner, reaction_ref[place, :])
            )
        side = split(jnp.concatenate(sides, 0))
        out_refs[number][...] = both_sides(x_ref, side, parts(y_ref), place_out) * scale


def inverse_kernel(core_ref, last_ref, kept_ref, came_ref, own_ref, x_ref, y_ref, out_ref, work_ref):
    modes = gather_halves(core_ref[0], work_ref, kept_ref, came_ref)
    former = jnp.where(last_ref[0] == 1, 1.0, 0.0)
    for place in row_halves(work_ref.shape[0]):
        out_ref[place, :] = former * own_ref[place, :] + both_sides(x_ref, modes, parts(y_ref), place)


def steps_kernel(odd_ref, entering_ref, kept_ref, came_ref, rate_ref, new_ref, sent_ref):
    odd = odd_ref[0] == 1
    kept, came, rate = kept_ref[...], came_ref[...], rate_ref[...]
    first = rate * (entering_ref[...] + jnp.where(odd, came, kept))
    second = rate * (first + jnp.where(odd, kept, came))
    new_ref[...] = jnp.where(odd, second, first)
    sent_ref[...] = jnp.where(odd, first, second)


def call(kernel, scalars, arrays, out_shapes, scratch=()):
    spec_scalar = pl.BlockSpec(memory_space=pltpu.SMEM)
    spec_array = pl.BlockSpec(memory_space=pltpu.VMEM)
    return pl.pallas_call(
        kernel,
        out_shape=[jax.ShapeDtypeStruct(shape, jnp.float32) for shape in out_shapes],
        in_specs=[spec_scalar] * len(scalars) + [spec_array] * len(arrays),
        out_specs=[spec_array] * len(out_shapes),
        scratch_shapes=[pltpu.VMEM(shape, jnp.float32) for shape in scratch],
        compiler_params=pltpu.CompilerParams(vmem_limit_bytes=16 * 1024 * 1024),
    )(*scalars, *arrays)


def swap(values, axis, mask):
    masks = mask if isinstance(mask, tuple) else (mask, mask)
    return lax.ppermute(values, axis, [(i, i ^ masks[i & 1]) for i in range(lax.axis_size(axis))])


def power(base, exponent):
    result = None
    while exponent:
        if exponent & 1:
            result = base if result is None else result * base
        base, exponent = base * base, exponent >> 1
    return result


def pick(options, index):
    result = options[0]
    for number in range(1, len(options)):
        result = jnp.where(index == number, options[number], result)
    return result


def scan_factors(rate, alpha, place, core, total):
    none = jnp.zeros_like(rate)
    pair = (pick([rate * rate, rate], place & 1), pick([rate, rate * rate], place & 1))
    all_masks, levels, reach = [], [], None
    bit, steps = 1, 2
    while steps < total:
        count = 4 if steps * 4 <= total else 2
        numbers = [(3, 3), (2, 1), (1, 2)] if count == 4 else [(1, 1)]
        masks = [(even << bit, odd << bit) for even, odd in numbers]
        if count == 2 and bit > 1:
            masks = [((1 << bit) | (1 << (bit - 1)),) * 2]
        factor = power(rate, steps)
        powers = [jnp.ones_like(rate)]
        for _ in range(count - 1):
            powers.append(powers[-1] * factor)
        mine = (place >> bit) & (count - 1)
        others = [mine ^ jnp.where(core == 1, odd, even) for even, odd in [(0, 0)] + numbers]
        join = [pick(powers[::-1], other) for other in others]
        enter = [pick([none] + powers, jnp.maximum(mine - other, 0)) for other in others]
        through = pick(powers, mine)
        bit, steps = bit + count.bit_length() - 1, steps * count
        if steps == total:
            round_trip = alpha / (1.0 - alpha * power(rate, total)) * through
            enter = [round_trip * one + two for one, two in zip(join, enter)]
        if reach is not None:
            enter = [reach * one for one in enter]
        reach = through if reach is None else reach * through
        all_masks.append(masks)
        levels.append((join, enter))
    pair, levels = lax.optimization_barrier((pair, levels))
    return pair, [(masks, *level) for masks, level in zip(all_masks, levels)]


def carry_in(kept, came, pair, levels, share):
    others = [swap(kept, "pair", 1), swap(came, "pair", 1)] if share else [None, None]
    carry = pair[0] * kept + pair[1] * came
    entering = jnp.zeros_like(carry)
    for masks, join, enter in levels[:-1]:
        pieces = [carry] + [swap(carry, "tm", mask) for mask in masks]
        carry = sum(one * piece for one, piece in zip(join, pieces))
        entering = entering + sum(one * piece for one, piece in zip(enter, pieces))
    carry = lax.optimization_barrier(carry)
    masks, _, enter = levels[-1]
    entering, others = lax.optimization_barrier((entering + enter[0] * carry, others))
    entering = entering + sum(one * swap(carry, "tm", mask) for one, mask in zip(enter[1:], masks))
    return lax.optimization_barrier((entering, others))


def on_device(fields, forcing, diffusion, reaction, wrap_factor, mean_diffusion, spectral_shift):
    total = lax.axis_size("tm")
    own, source = fields[0, 0], forcing[0, 0]
    grid_x, grid_y = own.shape
    half = grid_x // 2
    scale = 1.0 / (grid_x * grid_y)
    tables = cas_table(grid_x), cas_table(grid_y)
    group, step = lax.axis_index("pair"), lax.axis_index("tm")
    place = jnp.where(group == 1, total - 1 - step, step)
    other_place = total - 1 - place
    core = step & 1

    def scalar(value):
        return value.astype(jnp.int32).reshape(1)

    adjoint, side_of = scalar(group), scalar(core)
    odd, other_odd = scalar(place & 1), scalar(other_place & 1)
    last = [scalar(one == total - 1) for one in (place, place ^ 1)]
    other_last = [scalar(one == total - 1) for one in (other_place, other_place ^ 1)]
    eigen_x = lax.dynamic_slice_in_dim(eigenvalues(grid_x), core * half, half, 0)
    rate = 1.0 / (1.0 + spectral_shift + mean_diffusion * (eigen_x[:, None] + eigenvalues(grid_y)[None, :]))
    pair, levels = scan_factors(rate, wrap_factor, place, core, total)

    def own_side(number):
        (side,) = call(
            own_kernel,
            (mean_diffusion, spectral_shift, adjoint, last[number]),
            (fields_now[number], sources[number], diffusion, reaction),
            [own.shape],
        )
        return side

    def both_steps(odd, entering, kept, came):
        return call(steps_kernel, (odd,), (entering, kept, came, rate), [kept.shape] * 2)

    def inverse(number, kept, came):
        (field,) = call(
            inverse_kernel,
            (side_of, last[number]),
            (kept, came, fields_now[number], *tables),
            [own.shape],
            [own.shape],
        )
        return field

    partners = [swap(own, "pair", 1)]
    fields_now, sources = [own], [source]
    sides = [own_side(0)]
    if ITERS > 1:
        fields_now.append(swap(own, "tm", 1))
        sources.append(swap(source, "tm", 1))
    for iteration in range(ITERS):
        more = iteration + 1 < ITERS
        if iteration == 0:
            side, sent = call(
                functools.partial(first_kernel, scale),
                (adjoint, side_of),
                (sides[0], own, partners[0], reaction, *tables),
                [own.shape, (half, grid_y)],
            )
            came = swap(sent, "tm", 1)
            (kept,) = call(functools.partial(keep_kernel, scale), (side_of,), (side, *tables), [(half, grid_y)])
            if more:
                partners.append(swap(partners[0], "tm", 1))
        else:
            kept, came, *partners = call(
                functools.partial(later_kernel, scale),
                (adjoint, side_of, *other_last),
                (
                    reaction, *tables,
                    sides[0], fields_now[0], other_new, swap(other_sent, "tm", 1), partners[0],
                    sides[1], fields_now[1], other_sent, swap(other_new, "tm", 1), partners[1],
                ),
                [(half, grid_y)] * 2 + [own.shape] * (2 * more),
                [own.shape] * 2,
            )
        entering, other_sides = carry_in(kept, came, pair, levels, more)
        new, sent = both_steps(odd, entering, kept, came)
        if more:
            other_entering = swap(entering, "pair", 1)
            own_came, sibling_came = swap(sent, "tm", 1), swap(new, "tm", 1)
            fields_now = [inverse(0, new, own_came), inverse(1, sent, sibling_came)]
            sides = [own_side(0), own_side(1)]
            other_entering, sides = lax.optimization_barrier((other_entering, sides))
            other_new, other_sent = both_steps(other_odd, other_entering, *other_sides)
        else:
            fields_now = [inverse(0, new, swap(sent, "tm", 1))]
    own = fields_now[0]
    return own[None, None]


def solution(mesh):
    in_specs = (P("pair", "tm", None, None), P("pair", "tm", None, None), P(), P(), P(), P(), P())
    out_specs = P("pair", "tm", None, None)
    return jax.shard_map(
        on_device, mesh=mesh, in_specs=in_specs, out_specs=out_specs, check_vma=False
    )
```

```python
import functools
import math

import jax
import jax.numpy as jnp
import ml_dtypes
import numpy as np
from jax import lax
from jax.experimental import pallas as pl
from jax.experimental.pallas import tpu as pltpu
from jax.sharding import PartitionSpec as P

ITERS = 2

gamma_inv = 0.5


def cas_table(length):
    places = np.arange(length)
    angles = (places[:, None] * places[None, :] % length) * (2.0 * np.pi / length)
    table = np.cos(angles) + np.sin(angles)
    high = table.astype(ml_dtypes.bfloat16)
    low = (table - high.astype(np.float64)).astype(ml_dtypes.bfloat16)
    return jnp.asarray(np.stack([high, low]))


def eigenvalues(length):
    return jnp.asarray((4.0 * np.sin(np.arange(length) * (np.pi / length)) ** 2).astype(np.float32))


def split(values):
    high = values.astype(jnp.bfloat16)
    return high, (values - high.astype(jnp.float32)).astype(jnp.bfloat16)


def parts(table_ref):
    return table_ref[0], table_ref[1]


def product(left, right):
    def one(a, b):
        return jnp.dot(a, b, preferred_element_type=jnp.float32)

    return one(left[0], right[0]) + (one(left[0], right[1]) + one(left[1], right[0]))


def roll(values, shift, axis):
    return pltpu.roll(values, shift % values.shape[axis], axis)


def own_kernel(mean_ref, shift_ref, adjoint_ref, last_ref, own_ref, source_ref, diffusion_ref, reaction_ref, out_ref):
    last = last_ref[0] == 1
    mean = jnp.where(last, 0.0, mean_ref[0])
    shift = jnp.where(last, -1.0, shift_ref[0])
    cells, own = diffusion_ref[...], own_ref[...]
    east = 0.5 * (cells + roll(cells, -1, 0)) - mean
    north = 0.5 * (cells + roll(cells, -1, 1)) - mean
    flux_x = east * (roll(own, -1, 0) - own)
    flux_y = north * (roll(own, -1, 1) - own)
    spread = flux_x - roll(flux_x, 1, 0) + flux_y - roll(flux_y, 1, 1)
    cube = jnp.where(adjoint_ref[0] == 1, 0.0, 1.0) * (reaction_ref[...] * own * own * own)
    out_ref[...] = source_ref[...] + (spread + shift * own - cube)


def gather_halves(core, work_ref, kept_ref, came_ref):
    half = kept_ref.shape[0]
    work_ref[pl.ds(pl.multiple_of(core * half, half), half), :] = kept_ref[...]
    work_ref[pl.ds(pl.multiple_of((1 - core) * half, half), half), :] = came_ref[...]
    return split(work_ref[...])


def row_halves(count):
    return slice(0, count // 2), slice(count // 2, count)


def both_sides(x_ref, middle, y_table, place):
    return product(split(product((x_ref[0, place], x_ref[1, place]), middle)), y_table)


def half_rows(core, half):
    return pl.ds(pl.multiple_of(core * half, half), half)


def coupled(adjoint, side, own, partner, reaction):
    adjoint_part = 3.0 * reaction * partner * partner * own - partner
    return side - jnp.where(adjoint, adjoint_part, gamma_inv * partner)


def send_half(scale, core, side, x_ref, y_ref, send_ref):
    place = half_rows(1 - core, send_ref.shape[0])
    send_ref[...] = both_sides(x_ref, split(side), parts(y_ref), place) * scale


def keep_kernel(scale, core_ref, side_ref, x_ref, y_ref, keep_ref):
    place = half_rows(core_ref[0], keep_ref.shape[0])
    keep_ref[...] = both_sides(x_ref, split(side_ref[...]), parts(y_ref), place) * scale


def first_kernel(
    scale, adjoint_ref, core_ref, own_side_ref, own_ref, partner_ref, reaction_ref, x_ref, y_ref, side_ref, send_ref
):
    side = coupled(adjoint_ref[0] == 1, own_side_ref[...], own_ref[...], partner_ref[...], reaction_ref[...])
    side_ref[...] = side
    send_half(scale, core_ref[0], side, x_ref, y_ref, send_ref)


def later_kernel(
    scale, adjoint_ref, core_ref, partner_last_ref,
    own_side_ref, own_ref, kept_ref, came_ref, former_ref, reaction_ref, x_ref, y_ref,
    side_ref, send_ref, *refs,
):
    modes = gather_halves(core_ref[0], refs[-1], kept_ref, came_ref)
    former = jnp.where(partner_last_ref[0] == 1, 1.0, 0.0)
    sides = []
    for place in row_halves(own_ref.shape[0]):
        partner = former * former_ref[place, :] + both_sides(x_ref, modes, parts(y_ref), place)
        if len(refs) > 1:
            refs[0][place, :] = partner
        sides.append(
            coupled(adjoint_ref[0] == 1, own_side_ref[place, :], own_ref[place, :], partner, reaction_ref[place, :])
        )
        side_ref[place, :] = sides[-1]
    send_half(scale, core_ref[0], jnp.concatenate(sides, 0), x_ref, y_ref, send_ref)


def inverse_kernel(core_ref, last_ref, kept_ref, came_ref, own_ref, x_ref, y_ref, out_ref, work_ref):
    modes = gather_halves(core_ref[0], work_ref, kept_ref, came_ref)
    former = jnp.where(last_ref[0] == 1, 1.0, 0.0)
    for place in row_halves(work_ref.shape[0]):
        out_ref[place, :] = former * own_ref[place, :] + both_sides(x_ref, modes, parts(y_ref), place)


def steps_kernel(odd_ref, entering_ref, kept_ref, came_ref, rate_ref, new_ref, sent_ref):
    odd = odd_ref[0] == 1
    kept, came, rate = kept_ref[...], came_ref[...], rate_ref[...]
    first = rate * (entering_ref[...] + jnp.where(odd, came, kept))
    second = rate * (first + jnp.where(odd, kept, came))
    new_ref[...] = jnp.where(odd, second, first)
    sent_ref[...] = jnp.where(odd, first, second)


def call(kernel, scalars, arrays, out_shapes, scratch=(), flops=0):
    spec_scalar = pl.BlockSpec(memory_space=pltpu.SMEM)
    spec_array = pl.BlockSpec(memory_space=pltpu.VMEM)
    return pl.pallas_call(
        kernel,
        out_shape=[jax.ShapeDtypeStruct(shape, jnp.float32) for shape in out_shapes],
        in_specs=[spec_scalar] * len(scalars) + [spec_array] * len(arrays),
        out_specs=[spec_array] * len(out_shapes),
        scratch_shapes=[pltpu.VMEM(shape, jnp.float32) for shape in scratch],
        compiler_params=pltpu.CompilerParams(vmem_limit_bytes=16 * 1024 * 1024),
    )(*scalars, *arrays)


def swap(values, axis, mask):
    masks = mask if isinstance(mask, tuple) else (mask, mask)
    return lax.ppermute(values, axis, [(i, i ^ masks[i & 1]) for i in range(lax.axis_size(axis))])


def power(base, exponent):
    result = None
    while exponent:
        if exponent & 1:
            result = base if result is None else result * base
        base, exponent = base * base, exponent >> 1
    return result


def pick(options, index):
    result = options[0]
    for number in range(1, len(options)):
        result = jnp.where(index == number, options[number], result)
    return result


def scan_factors(rate, alpha, place, core, total):
    none = jnp.zeros_like(rate)
    pair = (pick([rate * rate, rate], place & 1), pick([rate, rate * rate], place & 1))
    all_masks, levels, reach = [], [], None
    bit, steps = 1, 2
    while steps < total:
        count = 4 if steps * 4 <= total else 2
        numbers = [(3, 3), (2, 1), (1, 2)] if count == 4 else [(1, 1)]
        masks = [(even << bit, odd << bit) for even, odd in numbers]
        if count == 2 and bit > 1:
            masks = [((1 << bit) | (1 << (bit - 1)),) * 2]
        factor = power(rate, steps)
        powers = [jnp.ones_like(rate)]
        for _ in range(count - 1):
            powers.append(powers[-1] * factor)
        mine = (place >> bit) & (count - 1)
        others = [mine ^ jnp.where(core == 1, odd, even) for even, odd in [(0, 0)] + numbers]
        join = [pick(powers[::-1], other) for other in others]
        enter = [pick([none] + powers, jnp.maximum(mine - other, 0)) for other in others]
        through = pick(powers, mine)
        bit, steps = bit + count.bit_length() - 1, steps * count
        if steps == total:
            round_trip = alpha / (1.0 - alpha * power(rate, total)) * through
            enter = [round_trip * one + two for one, two in zip(join, enter)]
        if reach is not None:
            enter = [reach * one for one in enter]
        reach = through if reach is None else reach * through
        all_masks.append(masks)
        levels.append((join, enter))
    pair, levels = lax.optimization_barrier((pair, levels))
    return pair, [(masks, *level) for masks, level in zip(all_masks, levels)]


def carry_in(kept, came, pair, levels, share):
    others = jnp.split(swap(jnp.concatenate([kept, came]), "pair", 1), 2) if share else [None, None]
    carry = pair[0] * kept + pair[1] * came
    entering = jnp.zeros_like(carry)
    for masks, join, enter in levels[:-1]:
        pieces = [carry] + [swap(carry, "tm", mask) for mask in masks]
        carry = sum(one * piece for one, piece in zip(join, pieces))
        entering = entering + sum(one * piece for one, piece in zip(enter, pieces))
    carry = lax.optimization_barrier(carry)
    masks, _, enter = levels[-1]
    entering, others = lax.optimization_barrier((entering + enter[0] * carry, others))
    entering = entering + sum(one * swap(carry, "tm", mask) for one, mask in zip(enter[1:], masks))
    return lax.optimization_barrier((entering, others))


def on_device(fields, forcing, diffusion, reaction, wrap_factor, mean_diffusion, spectral_shift):
    total = lax.axis_size("tm")
    own, source = fields[0, 0], forcing[0, 0]
    grid_x, grid_y = own.shape
    half = grid_x // 2
    scale = 1.0 / (grid_x * grid_y)
    tables = cas_table(grid_x), cas_table(grid_y)
    group, step = lax.axis_index("pair"), lax.axis_index("tm")
    place = jnp.where(group == 1, total - 1 - step, step)
    other_place = total - 1 - place
    core = step & 1

    def scalar(value):
        return value.astype(jnp.int32).reshape(1)

    adjoint, side_of = scalar(group), scalar(core)
    odd, other_odd = scalar(place & 1), scalar(other_place & 1)
    last, other_last = scalar(place == total - 1), scalar(other_place == total - 1)
    eigen_x = lax.dynamic_slice_in_dim(eigenvalues(grid_x), core * half, half, 0)
    rate = 1.0 / (1.0 + spectral_shift + mean_diffusion * (eigen_x[:, None] + eigenvalues(grid_y)[None, :]))
    pair, levels = scan_factors(rate, wrap_factor, place, core, total)

    def own_side(own):
        (side,) = call(
            own_kernel,
            (mean_diffusion, spectral_shift, adjoint, last),
            (own, source, diffusion, reaction),
            [own.shape],
        )
        return side

    def both_steps(odd, entering, kept, came):
        return call(steps_kernel, (odd,), (entering, kept, came, rate), [kept.shape] * 2)

    partner = [swap(own, "pair", 1)]
    side = own_side(own)
    for iteration in range(ITERS):
        more = iteration + 1 < ITERS
        if iteration == 0:
            side, sent = call(
                functools.partial(first_kernel, scale),
                (adjoint, side_of),
                (side, own, *partner, reaction, *tables),
                [own.shape, (half, grid_y)],
            )
        else:
            side, sent, *partner = call(
                functools.partial(later_kernel, scale),
                (adjoint, side_of, other_last),
                (side, own, other_kept, other_came, *partner, reaction, *tables),
                [own.shape, (half, grid_y)] + [own.shape] * more,
                [own.shape],
            )
        came = swap(sent, "tm", 1)
        (kept,) = call(functools.partial(keep_kernel, scale), (side_of,), (side, *tables), [(half, grid_y)])
        entering, other_sides = carry_in(kept, came, pair, levels, more)
        new, sent = both_steps(odd, entering, kept, came)
        if more:
            other_entering = swap(entering, "pair", 1)
        (own,) = call(
            inverse_kernel,
            (side_of, last),
            (new, swap(sent, "tm", 1), own, *tables),
            [own.shape],
            [own.shape],
        )
        if more:
            side = own_side(own)
            other_entering, side = lax.optimization_barrier((other_entering, side))
            other_kept, other_sent = both_steps(other_odd, other_entering, *other_sides)
            other_came = swap(other_sent, "tm", 1)
    return own[None, None]


def solution(mesh):
    in_specs = (P("pair", "tm", None, None), P("pair", "tm", None, None), P(), P(), P(), P(), P())
    out_specs = P("pair", "tm", None, None)
    return jax.shard_map(
        on_device, mesh=mesh, in_specs=in_specs, out_specs=out_specs, check_vma=False
    )
```

```python
import functools
import math

import jax
import jax.numpy as jnp
import ml_dtypes
import numpy as np
from jax import lax
from jax.experimental import pallas as pl
from jax.experimental.pallas import tpu as pltpu
from jax.sharding import PartitionSpec as P

ITERS = 2

gamma_inv = 0.5


def cas_table(length):
    places = np.arange(length)
    angles = (places[:, None] * places[None, :] % length) * (2.0 * np.pi / length)
    table = np.cos(angles) + np.sin(angles)
    high = table.astype(ml_dtypes.bfloat16)
    low = (table - high.astype(np.float64)).astype(ml_dtypes.bfloat16)
    return jnp.asarray(np.stack([high, low]))


def eigenvalues(length):
    return jnp.asarray((4.0 * np.sin(np.arange(length) * (np.pi / length)) ** 2).astype(np.float32))


def split(values):
    high = values.astype(jnp.bfloat16)
    return high, (values - high.astype(jnp.float32)).astype(jnp.bfloat16)


def parts(table_ref):
    return table_ref[0], table_ref[1]


def product(left, right):
    def one(a, b):
        return jnp.dot(a, b, preferred_element_type=jnp.float32)

    return one(left[0], right[0]) + (one(left[0], right[1]) + one(left[1], right[0]))


def roll(values, shift, axis):
    return pltpu.roll(values, shift % values.shape[axis], axis)


def own_kernel(mean_ref, shift_ref, adjoint_ref, last_ref, own_ref, source_ref, diffusion_ref, reaction_ref, out_ref):
    last = last_ref[0] == 1
    mean = jnp.where(last, 0.0, mean_ref[0])
    shift = jnp.where(last, -1.0, shift_ref[0])
    cells, own = diffusion_ref[...], own_ref[...]
    east = 0.5 * (cells + roll(cells, -1, 0)) - mean
    north = 0.5 * (cells + roll(cells, -1, 1)) - mean
    flux_x = east * (roll(own, -1, 0) - own)
    flux_y = north * (roll(own, -1, 1) - own)
    spread = flux_x - roll(flux_x, 1, 0) + flux_y - roll(flux_y, 1, 1)
    cube = jnp.where(adjoint_ref[0] == 1, 0.0, 1.0) * (reaction_ref[...] * own * own * own)
    out_ref[...] = source_ref[...] + (spread + shift * own - cube)


def gather_halves(core, work_ref, kept_ref, came_ref):
    half = kept_ref.shape[0]
    work_ref[pl.ds(pl.multiple_of(core * half, half), half), :] = kept_ref[...]
    work_ref[pl.ds(pl.multiple_of((1 - core) * half, half), half), :] = came_ref[...]
    return split(work_ref[...])


def row_halves(count):
    return slice(0, count // 2), slice(count // 2, count)


def both_sides(x_ref, middle, y_table, place):
    return product(split(product((x_ref[0, place], x_ref[1, place]), middle)), y_table)


def half_rows(core, half):
    return pl.ds(pl.multiple_of(core * half, half), half)


def coupled(adjoint, side, own, partner, reaction):
    adjoint_part = 3.0 * reaction * partner * partner * own - partner
    return side - jnp.where(adjoint, adjoint_part, gamma_inv * partner)


def send_half(scale, core, side, x_ref, y_ref, send_ref):
    place = half_rows(1 - core, send_ref.shape[0])
    send_ref[...] = both_sides(x_ref, split(side), parts(y_ref), place) * scale


def keep_kernel(scale, core_ref, side_ref, x_ref, y_ref, keep_ref):
    place = half_rows(core_ref[0], keep_ref.shape[0])
    keep_ref[...] = both_sides(x_ref, split(side_ref[...]), parts(y_ref), place) * scale


def first_kernel(
    scale, adjoint_ref, core_ref, own_side_ref, own_ref, partner_ref, reaction_ref, x_ref, y_ref, side_ref, send_ref
):
    side = coupled(adjoint_ref[0] == 1, own_side_ref[...], own_ref[...], partner_ref[...], reaction_ref[...])
    side_ref[...] = side
    send_half(scale, core_ref[0], side, x_ref, y_ref, send_ref)


def later_kernel(
    scale, adjoint_ref, core_ref, partner_last_ref,
    own_side_ref, own_ref, kept_ref, came_ref, former_ref, reaction_ref, x_ref, y_ref,
    side_ref, send_ref, *refs,
):
    modes = gather_halves(core_ref[0], refs[-1], kept_ref, came_ref)
    former = jnp.where(partner_last_ref[0] == 1, 1.0, 0.0)
    sides = []
    for place in row_halves(own_ref.shape[0]):
        partner = former * former_ref[place, :] + both_sides(x_ref, modes, parts(y_ref), place)
        if len(refs) > 1:
            refs[0][place, :] = partner
        sides.append(
            coupled(adjoint_ref[0] == 1, own_side_ref[place, :], own_ref[place, :], partner, reaction_ref[place, :])
        )
        side_ref[place, :] = sides[-1]
    send_half(scale, core_ref[0], jnp.concatenate(sides, 0), x_ref, y_ref, send_ref)


def inverse_kernel(core_ref, last_ref, kept_ref, came_ref, own_ref, x_ref, y_ref, out_ref, work_ref):
    modes = gather_halves(core_ref[0], work_ref, kept_ref, came_ref)
    former = jnp.where(last_ref[0] == 1, 1.0, 0.0)
    for place in row_halves(work_ref.shape[0]):
        out_ref[place, :] = former * own_ref[place, :] + both_sides(x_ref, modes, parts(y_ref), place)


def steps_kernel(odd_ref, entering_ref, kept_ref, came_ref, rate_ref, new_ref, sent_ref):
    odd = odd_ref[0] == 1
    kept, came, rate = kept_ref[...], came_ref[...], rate_ref[...]
    first = rate * (entering_ref[...] + jnp.where(odd, came, kept))
    second = rate * (first + jnp.where(odd, kept, came))
    new_ref[...] = jnp.where(odd, second, first)
    sent_ref[...] = jnp.where(odd, first, second)


def own_steps_kernel(odd_ref, base_ref, kept_ref, came_ref, rate_ref, *refs):
    entering_ref, new_ref, sent_ref = refs[-3:]
    entering = base_ref[...]
    for factor_ref, piece_ref in zip(refs[:-3:2], refs[1:-3:2]):
        entering = entering + factor_ref[...] * piece_ref[...]
    entering_ref[...] = entering
    steps_kernel(odd_ref, entering_ref, kept_ref, came_ref, rate_ref, new_ref, sent_ref)


def call(kernel, scalars, arrays, out_shapes, scratch=()):
    spec_scalar = pl.BlockSpec(memory_space=pltpu.SMEM)
    spec_array = pl.BlockSpec(memory_space=pltpu.VMEM)
    return pl.pallas_call(
        kernel,
        out_shape=[jax.ShapeDtypeStruct(shape, jnp.float32) for shape in out_shapes],
        in_specs=[spec_scalar] * len(scalars) + [spec_array] * len(arrays),
        out_specs=[spec_array] * len(out_shapes),
        scratch_shapes=[pltpu.VMEM(shape, jnp.float32) for shape in scratch],
        compiler_params=pltpu.CompilerParams(vmem_limit_bytes=16 * 1024 * 1024),
    )(*scalars, *arrays)


def swap(values, axis, mask):
    masks = mask if isinstance(mask, tuple) else (mask, mask)
    return lax.ppermute(values, axis, [(i, i ^ masks[i & 1]) for i in range(lax.axis_size(axis))])


def power(base, exponent):
    result = None
    while exponent:
        if exponent & 1:
            result = base if result is None else result * base
        base, exponent = base * base, exponent >> 1
    return result


def pick(options, index):
    result = options[0]
    for number in range(1, len(options)):
        result = jnp.where(index == number, options[number], result)
    return result


def scan_factors(rate, alpha, place, core, total):
    none = jnp.zeros_like(rate)
    pair = (pick([rate * rate, rate], place & 1), pick([rate, rate * rate], place & 1))
    all_masks, levels, reach = [], [], None
    bit, steps = 1, 2
    while steps < total:
        count = 4 if steps * 4 <= total else 2
        numbers = [(3, 3), (2, 1), (1, 2)] if count == 4 else [(1, 1)]
        masks = [(even << bit, odd << bit) for even, odd in numbers]
        if count == 2 and bit > 1:
            masks = [((1 << bit) | (1 << (bit - 1)),) * 2]
        factor = power(rate, steps)
        powers = [jnp.ones_like(rate)]
        for _ in range(count - 1):
            powers.append(powers[-1] * factor)
        mine = (place >> bit) & (count - 1)
        others = [mine ^ jnp.where(core == 1, odd, even) for even, odd in [(0, 0)] + numbers]
        join = [pick(powers[::-1], other) for other in others]
        enter = [pick([none] + powers, jnp.maximum(mine - other, 0)) for other in others]
        through = pick(powers, mine)
        bit, steps = bit + count.bit_length() - 1, steps * count
        if steps == total:
            round_trip = alpha / (1.0 - alpha * power(rate, total)) * through
            enter = [round_trip * one + two for one, two in zip(join, enter)]
        if reach is not None:
            enter = [reach * one for one in enter]
        reach = through if reach is None else reach * through
        all_masks.append(masks)
        levels.append((join, enter))
    pair, levels = lax.optimization_barrier((pair, levels))
    return pair, [(masks, *level) for masks, level in zip(all_masks, levels)]


def carry_in(kept, came, pair, levels, share):
    others = [swap(kept, "pair", 1), swap(came, "pair", 1)] if share else [None, None]
    carry = pair[0] * kept + pair[1] * came
    entering = jnp.zeros_like(carry)
    for masks, join, enter in levels[:-1]:
        pieces = [carry] + [swap(carry, "tm", mask) for mask in masks]
        carry = sum(one * piece for one, piece in zip(join, pieces))
        entering = entering + sum(one * piece for one, piece in zip(enter, pieces))
    carry = lax.optimization_barrier(carry)
    masks, _, enter = levels[-1]
    entering, others = lax.optimization_barrier((entering + enter[0] * carry, others))
    last_terms = [(one, swap(carry, "tm", mask)) for one, mask in zip(enter[1:], masks)]
    last_terms, others = lax.optimization_barrier((last_terms, others))
    return entering, last_terms, others


def on_device(fields, forcing, diffusion, reaction, wrap_factor, mean_diffusion, spectral_shift):
    total = lax.axis_size("tm")
    own, source = fields[0, 0], forcing[0, 0]
    grid_x, grid_y = own.shape
    half = grid_x // 2
    scale = 1.0 / (grid_x * grid_y)
    tables = cas_table(grid_x), cas_table(grid_y)
    group, step = lax.axis_index("pair"), lax.axis_index("tm")
    place = jnp.where(group == 1, total - 1 - step, step)
    other_place = total - 1 - place
    core = step & 1

    def scalar(value):
        return value.astype(jnp.int32).reshape(1)

    adjoint, side_of = scalar(group), scalar(core)
    odd, other_odd = scalar(place & 1), scalar(other_place & 1)
    last, other_last = scalar(place == total - 1), scalar(other_place == total - 1)
    eigen_x = lax.dynamic_slice_in_dim(eigenvalues(grid_x), core * half, half, 0)
    rate = 1.0 / (1.0 + spectral_shift + mean_diffusion * (eigen_x[:, None] + eigenvalues(grid_y)[None, :]))
    pair, levels = scan_factors(rate, wrap_factor, place, core, total)

    def own_side(own):
        (side,) = call(
            own_kernel,
            (mean_diffusion, spectral_shift, adjoint, last),
            (own, source, diffusion, reaction),
            [own.shape],
        )
        return side

    def both_steps(odd, entering, kept, came):
        return call(steps_kernel, (odd,), (entering, kept, came, rate), [kept.shape] * 2)

    partner = [swap(own, "pair", 1)]
    side = own_side(own)
    for iteration in range(ITERS):
        more = iteration + 1 < ITERS
        if iteration == 0:
            side, sent = call(
                functools.partial(first_kernel, scale),
                (adjoint, side_of),
                (side, own, *partner, reaction, *tables),
                [own.shape, (half, grid_y)],
            )
        else:
            side, sent, *partner = call(
                functools.partial(later_kernel, scale),
                (adjoint, side_of, other_last),
                (side, own, other_kept, other_came, *partner, reaction, *tables),
                [own.shape, (half, grid_y)] + [own.shape] * more,
                [own.shape],
            )
        came = swap(sent, "tm", 1)
        (kept,) = call(functools.partial(keep_kernel, scale), (side_of,), (side, *tables), [(half, grid_y)])
        base, last_terms, other_sides = carry_in(kept, came, pair, levels, more)
        terms = [array for term in last_terms for array in term]
        entering, new, sent = call(
            own_steps_kernel, (odd,), (base, kept, came, rate, *terms), [kept.shape] * 3
        )
        if more:
            other_entering = swap(entering, "pair", 1)
        (own,) = call(
            inverse_kernel,
            (side_of, last),
            (new, swap(sent, "tm", 1), own, *tables),
            [own.shape],
            [own.shape],
        )
        if more:
            side = own_side(own)
            other_entering, side = lax.optimization_barrier((other_entering, side))
            other_kept, other_sent = both_steps(other_odd, other_entering, *other_sides)
            other_came = swap(other_sent, "tm", 1)
    return own[None, None]


def solution(mesh):
    in_specs = (P("pair", "tm", None, None), P("pair", "tm", None, None), P(), P(), P(), P(), P())
    out_specs = P("pair", "tm", None, None)
    return jax.shard_map(
        on_device, mesh=mesh, in_specs=in_specs, out_specs=out_specs, check_vma=False
    )
```

```python
import functools
import math

import jax
import jax.numpy as jnp
import ml_dtypes
import numpy as np
from jax import lax
from jax.experimental import pallas as pl
from jax.experimental.pallas import tpu as pltpu
from jax.sharding import PartitionSpec as P

ITERS = 2

gamma_inv = 0.5


def cas_table(length):
    places = np.arange(length)
    angles = (places[:, None] * places[None, :] % length) * (2.0 * np.pi / length)
    table = np.cos(angles) + np.sin(angles)
    high = table.astype(ml_dtypes.bfloat16)
    low = (table - high.astype(np.float64)).astype(ml_dtypes.bfloat16)
    return jnp.asarray(np.stack([high, low]))


def eigenvalues(length):
    return jnp.asarray((4.0 * np.sin(np.arange(length) * (np.pi / length)) ** 2).astype(np.float32))


def split(values):
    high = values.astype(jnp.bfloat16)
    return high, (values - high.astype(jnp.float32)).astype(jnp.bfloat16)


def parts(table_ref):
    return table_ref[0], table_ref[1]


def product(left, right):
    def one(a, b):
        return jnp.dot(a, b, preferred_element_type=jnp.float32)

    return one(left[0], right[0]) + (one(left[0], right[1]) + one(left[1], right[0]))


def roll(values, shift, axis):
    return pltpu.roll(values, shift % values.shape[axis], axis)


def own_kernel(mean_ref, shift_ref, adjoint_ref, last_ref, own_ref, source_ref, diffusion_ref, reaction_ref, out_ref):
    last = last_ref[0] == 1
    mean = jnp.where(last, 0.0, mean_ref[0])
    shift = jnp.where(last, -1.0, shift_ref[0])
    cells, own = diffusion_ref[...], own_ref[...]
    east = 0.5 * (cells + roll(cells, -1, 0)) - mean
    north = 0.5 * (cells + roll(cells, -1, 1)) - mean
    flux_x = east * (roll(own, -1, 0) - own)
    flux_y = north * (roll(own, -1, 1) - own)
    spread = flux_x - roll(flux_x, 1, 0) + flux_y - roll(flux_y, 1, 1)
    cube = jnp.where(adjoint_ref[0] == 1, 0.0, 1.0) * (reaction_ref[...] * own * own * own)
    out_ref[...] = source_ref[...] + (spread + shift * own - cube)


def gather_halves(core, work_ref, kept_ref, came_ref):
    half = kept_ref.shape[0]
    work_ref[pl.ds(pl.multiple_of(core * half, half), half), :] = kept_ref[...]
    work_ref[pl.ds(pl.multiple_of((1 - core) * half, half), half), :] = came_ref[...]
    return split(work_ref[...])


def row_halves(count):
    return slice(0, count // 2), slice(count // 2, count)


def both_sides(x_ref, middle, y_table, place):
    return product(split(product((x_ref[0, place], x_ref[1, place]), middle)), y_table)


def half_rows(core, half):
    return pl.ds(pl.multiple_of(core * half, half), half)


def coupled(adjoint, side, own, partner, reaction):
    adjoint_part = 3.0 * reaction * partner * partner * own - partner
    return side - jnp.where(adjoint, adjoint_part, gamma_inv * partner)


def send_half(scale, core, side, x_ref, y_ref, send_ref):
    place = half_rows(1 - core, send_ref.shape[0])
    send_ref[...] = both_sides(x_ref, split(side), parts(y_ref), place) * scale


def keep_kernel(scale, core_ref, side_ref, x_ref, y_ref, keep_ref):
    place = half_rows(core_ref[0], keep_ref.shape[0])
    keep_ref[...] = both_sides(x_ref, split(side_ref[...]), parts(y_ref), place) * scale


def first_kernel(
    scale, adjoint_ref, core_ref, own_side_ref, own_ref, partner_ref, reaction_ref, x_ref, y_ref, side_ref, send_ref
):
    side = coupled(adjoint_ref[0] == 1, own_side_ref[...], own_ref[...], partner_ref[...], reaction_ref[...])
    side_ref[...] = side
    send_half(scale, core_ref[0], side, x_ref, y_ref, send_ref)


def later_kernel(
    scale, adjoint_ref, core_ref, partner_last_ref,
    own_side_ref, own_ref, kept_ref, came_ref, former_ref, reaction_ref, x_ref, y_ref,
    side_ref, send_ref, *refs,
):
    modes = gather_halves(core_ref[0], refs[-1], kept_ref, came_ref)
    former = jnp.where(partner_last_ref[0] == 1, 1.0, 0.0)
    sides = []
    for place in row_halves(own_ref.shape[0]):
        partner = former * former_ref[place, :] + both_sides(x_ref, modes, parts(y_ref), place)
        if len(refs) > 1:
            refs[0][place, :] = partner
        sides.append(
            coupled(adjoint_ref[0] == 1, own_side_ref[place, :], own_ref[place, :], partner, reaction_ref[place, :])
        )
        side_ref[place, :] = sides[-1]
    send_half(scale, core_ref[0], jnp.concatenate(sides, 0), x_ref, y_ref, send_ref)


def inverse_kernel(core_ref, last_ref, kept_ref, came_ref, own_ref, x_ref, y_ref, out_ref, work_ref):
    modes = gather_halves(core_ref[0], work_ref, kept_ref, came_ref)
    former = jnp.where(last_ref[0] == 1, 1.0, 0.0)
    for place in row_halves(work_ref.shape[0]):
        out_ref[place, :] = former * own_ref[place, :] + both_sides(x_ref, modes, parts(y_ref), place)


def final_kernel(
    core_ref, last_ref, kept_ref, came_ref, own_ref, x_ref, y_ref, out_ref, work_ref, field_ref, semaphores
):
    modes = gather_halves(core_ref[0], work_ref, kept_ref, came_ref)
    former = jnp.where(last_ref[0] == 1, 1.0, 0.0)
    copies = []
    for number, place in enumerate(row_halves(work_ref.shape[0])):
        field_ref[place, :] = former * own_ref[place, :] + both_sides(x_ref, modes, parts(y_ref), place)
        copies.append(pltpu.make_async_copy(field_ref.at[place], out_ref.at[place], semaphores.at[number]))
        copies[-1].start()
    for copy in copies:
        copy.wait()


def steps_kernel(odd_ref, entering_ref, kept_ref, came_ref, rate_ref, new_ref, sent_ref):
    odd = odd_ref[0] == 1
    kept, came, rate = kept_ref[...], came_ref[...], rate_ref[...]
    first = rate * (entering_ref[...] + jnp.where(odd, came, kept))
    second = rate * (first + jnp.where(odd, kept, came))
    new_ref[...] = jnp.where(odd, second, first)
    sent_ref[...] = jnp.where(odd, first, second)


def call(kernel, scalars, arrays, out_shapes, scratch=(), copies=0):
    spec_scalar = pl.BlockSpec(memory_space=pltpu.SMEM)
    spec_array = pl.BlockSpec(memory_space=pltpu.VMEM)
    return pl.pallas_call(
        kernel,
        out_shape=[jax.ShapeDtypeStruct(shape, jnp.float32) for shape in out_shapes],
        in_specs=[spec_scalar] * len(scalars) + [spec_array] * len(arrays),
        out_specs=[pl.BlockSpec(memory_space=pl.ANY) if copies else spec_array] * len(out_shapes),
        scratch_shapes=[pltpu.VMEM(shape, jnp.float32) for shape in scratch]
        + [pltpu.SemaphoreType.DMA((copies,))] * (copies > 0),
        compiler_params=pltpu.CompilerParams(vmem_limit_bytes=16 * 1024 * 1024),
    )(*scalars, *arrays)


def swap(values, axis, mask):
    masks = mask if isinstance(mask, tuple) else (mask, mask)
    return lax.ppermute(values, axis, [(i, i ^ masks[i & 1]) for i in range(lax.axis_size(axis))])


def power(base, exponent):
    result = None
    while exponent:
        if exponent & 1:
            result = base if result is None else result * base
        base, exponent = base * base, exponent >> 1
    return result


def pick(options, index):
    result = options[0]
    for number in range(1, len(options)):
        result = jnp.where(index == number, options[number], result)
    return result


def scan_factors(rate, alpha, place, core, total):
    none = jnp.zeros_like(rate)
    pair = (pick([rate * rate, rate], place & 1), pick([rate, rate * rate], place & 1))
    all_masks, levels, reach = [], [], None
    bit, steps = 1, 2
    while steps < total:
        count = 4 if steps * 4 <= total else 2
        numbers = [(3, 3), (2, 1), (1, 2)] if count == 4 else [(1, 1)]
        masks = [(even << bit, odd << bit) for even, odd in numbers]
        if count == 2 and bit > 1:
            masks = [((1 << bit) | (1 << (bit - 1)),) * 2]
        factor = power(rate, steps)
        powers = [jnp.ones_like(rate)]
        for _ in range(count - 1):
            powers.append(powers[-1] * factor)
        mine = (place >> bit) & (count - 1)
        others = [mine ^ jnp.where(core == 1, odd, even) for even, odd in [(0, 0)] + numbers]
        join = [pick(powers[::-1], other) for other in others]
        enter = [pick([none] + powers, jnp.maximum(mine - other, 0)) for other in others]
        through = pick(powers, mine)
        bit, steps = bit + count.bit_length() - 1, steps * count
        if steps == total:
            round_trip = alpha / (1.0 - alpha * power(rate, total)) * through
            enter = [round_trip * one + two for one, two in zip(join, enter)]
        if reach is not None:
            enter = [reach * one for one in enter]
        reach = through if reach is None else reach * through
        all_masks.append(masks)
        levels.append((join, enter))
    pair, levels = lax.optimization_barrier((pair, levels))
    return pair, [(masks, *level) for masks, level in zip(all_masks, levels)]


def carry_in(kept, came, pair, levels, share):
    others = [swap(kept, "pair", 1), swap(came, "pair", 1)] if share else [None, None]
    carry = pair[0] * kept + pair[1] * came
    entering = jnp.zeros_like(carry)
    for masks, join, enter in levels[:-1]:
        pieces = [carry] + [swap(carry, "tm", mask) for mask in masks]
        carry = sum(one * piece for one, piece in zip(join, pieces))
        entering = entering + sum(one * piece for one, piece in zip(enter, pieces))
    carry = lax.optimization_barrier(carry)
    masks, _, enter = levels[-1]
    entering, others = lax.optimization_barrier((entering + enter[0] * carry, others))
    entering = entering + sum(one * swap(carry, "tm", mask) for one, mask in zip(enter[1:], masks))
    return lax.optimization_barrier((entering, others))


def on_device(fields, forcing, diffusion, reaction, wrap_factor, mean_diffusion, spectral_shift):
    total = lax.axis_size("tm")
    own, source = fields[0, 0], forcing[0, 0]
    grid_x, grid_y = own.shape
    half = grid_x // 2
    scale = 1.0 / (grid_x * grid_y)
    tables = cas_table(grid_x), cas_table(grid_y)
    group, step = lax.axis_index("pair"), lax.axis_index("tm")
    place = jnp.where(group == 1, total - 1 - step, step)
    other_place = total - 1 - place
    core = step & 1

    def scalar(value):
        return value.astype(jnp.int32).reshape(1)

    adjoint, side_of = scalar(group), scalar(core)
    odd, other_odd = scalar(place & 1), scalar(other_place & 1)
    last, other_last = scalar(place == total - 1), scalar(other_place == total - 1)
    eigen_x = lax.dynamic_slice_in_dim(eigenvalues(grid_x), core * half, half, 0)
    rate = 1.0 / (1.0 + spectral_shift + mean_diffusion * (eigen_x[:, None] + eigenvalues(grid_y)[None, :]))
    pair, levels = scan_factors(rate, wrap_factor, place, core, total)

    def own_side(own):
        (side,) = call(
            own_kernel,
            (mean_diffusion, spectral_shift, adjoint, last),
            (own, source, diffusion, reaction),
            [own.shape],
        )
        return side

    def both_steps(odd, entering, kept, came):
        return call(steps_kernel, (odd,), (entering, kept, came, rate), [kept.shape] * 2)

    partner = [swap(own, "pair", 1)]
    side = own_side(own)
    for iteration in range(ITERS):
        more = iteration + 1 < ITERS
        if iteration == 0:
            side, sent = call(
                functools.partial(first_kernel, scale),
                (adjoint, side_of),
                (side, own, *partner, reaction, *tables),
                [own.shape, (half, grid_y)],
            )
        else:
            side, sent, *partner = call(
                functools.partial(later_kernel, scale),
                (adjoint, side_of, other_last),
                (side, own, other_kept, other_came, *partner, reaction, *tables),
                [own.shape, (half, grid_y)] + [own.shape] * more,
                [own.shape],
            )
        came = swap(sent, "tm", 1)
        (kept,) = call(functools.partial(keep_kernel, scale), (side_of,), (side, *tables), [(half, grid_y)])
        entering, other_sides = carry_in(kept, came, pair, levels, more)
        new, sent = both_steps(odd, entering, kept, came)
        if more:
            other_entering = swap(entering, "pair", 1)
        (own,) = call(
            inverse_kernel if more else final_kernel,
            (side_of, last),
            (new, swap(sent, "tm", 1), own, *tables),
            [own.shape],
            [own.shape] * (1 if more else 2),
            0 if more else 2,
        )
        if more:
            side = own_side(own)
            other_entering, side = lax.optimization_barrier((other_entering, side))
            other_kept, other_sent = both_steps(other_odd, other_entering, *other_sides)
            other_came = swap(other_sent, "tm", 1)
    return own[None, None]


def solution(mesh):
    in_specs = (P("pair", "tm", None, None), P("pair", "tm", None, None), P(), P(), P(), P(), P())
    out_specs = P("pair", "tm", None, None)
    return jax.shard_map(
        on_device, mesh=mesh, in_specs=in_specs, out_specs=out_specs, check_vma=False
    )
```
